512 devices in a mesh: users: 128 (over z, y, core), heads: 4 (over x).
Axes of the slice: x: 4, y: 8, z: 8, core: 2. Of those that a mesh axis runs over, the one named last changes fastest.
Arguments:
- events: bfloat16 [32768, 1024], P('users', 'heads'), may hold values from -6 to 6
- event_owner: int32 [32768, 1], P('users'), may hold values from 0 to 127; in each aligned block of 256 rows (0 to 255, 256 to 511, ...) at most 4 rows name the same one
- event_user: int32 [32768], P('users'), may hold values from 0 to 1
- cache_keys: bfloat16 [128, 2, 512, 1024], P('users', None, None, 'heads'), may hold values from -250 to 250
- cache_values: bfloat16 [128, 2, 512, 1024], P('users', None, None, 'heads'), may hold values from -6 to 6
- cache_len: int32 [128, 2], P('users'), may hold values from 256 to 512
- user_rank: int32 [128, 2], P('users'), may hold values from 0 to 127
- norm_gain: float32 [1024], replicated, may hold values from 0.5 to 1.5
- w_query: bfloat16 [1024, 1024], P(None, 'heads'), may hold values from -0.1875 to 0.1875
- w_key: bfloat16 [1024, 1024], P(None, 'heads'), may hold values from -0.1875 to 0.1875
- w_value: bfloat16 [1024, 1024], P(None, 'heads'), may hold values from -0.1875 to 0.1875
- w_out: bfloat16 [1024, 1024], P('heads'), may hold values from -0.1875 to 0.1875
Outputs:
- refreshed: bfloat16 [128, 512, 1024], P('users', None, 'heads')
- ranked: bfloat16 [128, 256, 1024], P('users', None, 'heads')
The draws below stay inside these ranges and needn't reach their ends.
Inputs may be any that keep to these rules, and one draw needn't show every extreme that they name: `event_owner`: in the rows of one index of users, no owner is named more than 4 times, a bound that some block reaches.
All inputs are finite; a program needn't handle non-finite values.
Results may differ from the reference program's by a relative error of at most 0.012.
Values may be sent and summed in bfloat16 or wider, within the bound.
No kernel may reach another device: no remote copies, remote signals or barrier semaphores. Data moves between devices by JAX's collectives and lax.ppermute only.
A program may use at most 64 MiB of HBM per device.

```python
import math
import jax
import jax.numpy as jnp
import numpy as np
from jax import lax

D = 1024
HEAD_DIM = 64
EV_DEV = 256
U_DEV = 2
CACHE = 512
CAP = 4
EVENTS = 32768
N_USERS = 128


def draw_cache_len(key, part):
    key = jax.random.fold_in(key, 11)
    first, second = jax.random.split(key)
    lengths = jax.random.randint(first, (N_USERS * U_DEV,), CACHE // 2, CACHE + 1)
    spot = jax.random.randint(second, (), 0, N_USERS * U_DEV)
    lengths = jnp.where(jnp.arange(N_USERS * U_DEV) == spot, CACHE, lengths)
    return lengths.reshape(N_USERS, U_DEV).astype(jnp.int32)


def draw_cache_keys(key, part):
    key = jax.random.fold_in(key, 23)
    keys = jax.random.split(key, 1)
    shape = (N_USERS, U_DEV, CACHE, D)
    base = jnp.clip(jax.random.normal(keys[0], shape, jnp.float32), -6.0, 6.0)
    return base.astype(jnp.bfloat16)


def touch_ends(result, rng, low, high):
    shape = result.shape
    index_at = [jax.random.randint(jax.random.fold_in(rng, axis), (), 0, shape[axis]) for axis in range(len(shape))]
    result = result.at[tuple(index_at)].set(low)
    longest = shape.index(max(shape))
    index_at[longest] = (index_at[longest] + 1) % shape[longest]
    return result.at[tuple(index_at)].set(high)


def block_levels(stream_key, shape, cuts, least, top_value):
    gain = 1.0
    for axis_at, parts in cuts:
        heights = jax.random.uniform(jax.random.fold_in(jax.random.fold_in(stream_key, 6), axis_at), (parts,), jnp.float32, least / len(cuts), top_value / len(cuts))
        gain = gain * jnp.repeat(jnp.exp(heights), shape[axis_at] // parts).reshape((-1,) + (1,) * (len(shape) - 1 - axis_at))
    return gain


def deal_out(stream_key, own, number, rows, count, top, limit, skew):
    ranking = jax.random.permutation(stream_key, count)
    heavy_load, ordinary = portions_of(count, rows * top, limit, skew, True), portions_of(count, rows * top, limit, skew, False)
    places = jnp.arange(count)

    def named(tallies, turn):
        used = int((tallies > 0).sum())
        fixed = max(1, used // 4)
        moved = fixed + (places - fixed + turn * (used - fixed)) % max(1, count - fixed)
        return jnp.zeros((count,), jnp.int32).at[ranking[jnp.where(places < fixed, places, moved)]].set(jnp.asarray(tallies, jnp.int32))

    tallies = jnp.where(number % 4 == 0, named(heavy_load, number // 4), named(ordinary, number - number // 4 - 1))
    mixed = jax.random.permutation(jax.random.fold_in(own, 3), count)
    giver, sink = mixed[0:count // 2 * 2:2], mixed[1:count // 2 * 2:2]
    room = jnp.minimum(tallies[giver] - 1, limit - tallies[sink]) // 2
    room = jnp.where((giver == ranking[0]) | (sink == ranking[0]) | (tallies[sink] == 0), 0, jnp.maximum(room, 0))
    moved = jax.random.randint(jax.random.fold_in(own, 4), (count // 2,), 0, 1 << 20) % (room + 1)
    tallies = tallies.at[giver].add(-moved).at[sink].add(moved)
    members = jnp.searchsorted(jnp.cumsum(tallies), jnp.arange(rows * top), side="right").astype(jnp.int32)
    grid = members.reshape(top, rows).T
    grid = grid[jax.random.permutation(jax.random.fold_in(own, 1), rows)]
    turn = jax.random.randint(jax.random.fold_in(own, 2), (rows, 1), 0, top)
    return jnp.take_along_axis(grid, (jnp.arange(top)[None, :] + turn) % top, axis=1)


def portions_of(amount, total, bound, skew, full):
    loads = [(1 << 20) // math.isqrt(rank ** skew) + 1 for rank in range(1, amount + 1)]
    largest = bound if full else min(bound, max(-(-total // amount), total * loads[0] // sum(loads)))
    least = 1 if total - largest >= amount - 1 else 0
    holding, rest = [largest] + [least] * (amount - 1), total - largest - least * (amount - 1)
    while rest > 0:
        free = [i for i in range(1, amount) if holding[i] < largest] or [i for i in range(1, amount) if holding[i] < bound]
        pool, remaining = sum([loads[i] for i in free]), rest
        for i in free:
            addition = min(bound - holding[i], max(1, remaining * loads[i] // pool), rest)
            holding[i] = holding[i] + addition
            rest = rest - addition
    return np.array(holding)


def gaussian(key, shape, deviation, limit, cuts=(), kind=jnp.bfloat16):
    entries = deviation * jax.random.normal(key, shape, jnp.float32)
    if cuts:
        entries = entries * block_levels(key, shape, cuts, -0.22, 0.18)
    return jnp.clip(entries, -limit, limit).astype(kind)


def setup_inputs(seed: int = 0) -> dict:
    arg_keys = jax.random.split(jax.random.key(seed), 13)
    events = gaussian(arg_keys[0], (EVENTS, D), 1.0, 6.0, ((0, 128), (1, 4)))
    event_owner_keys = jax.random.split(jax.random.fold_in(arg_keys[1], 1), EVENTS // EV_DEV)
    event_owner_turns = jax.random.permutation(jax.random.fold_in(arg_keys[1], 3), EVENTS // EV_DEV)
    event_owner = jax.vmap(lambda own, number: deal_out(jax.random.fold_in(arg_keys[1], 2), own, number, EV_DEV, N_USERS, 1, CAP, 2))(event_owner_keys, event_owner_turns).reshape((EVENTS, 1))
    event_user = touch_ends(jax.random.randint(arg_keys[2], (EVENTS,), 0, U_DEV), jax.random.fold_in(arg_keys[2], 1), 0, U_DEV - 1).astype(jnp.int32)
    cache_keys = draw_cache_keys(jax.random.fold_in(arg_keys[12], 71), 0)
    cache_values = gaussian(arg_keys[4], (N_USERS, U_DEV, CACHE, D), 1.0, 6.0, ((0, 128), (3, 4)))
    cache_len = draw_cache_len(jax.random.fold_in(arg_keys[12], 71), 0)
    user_rank = touch_ends(jax.random.randint(arg_keys[6], (N_USERS, U_DEV), 0, N_USERS), jax.random.fold_in(arg_keys[6], 1), 0, N_USERS - 1).astype(jnp.int32)
    norm_gain = jnp.clip(1.0 + 0.1 * jax.random.normal(arg_keys[7], (D,), jnp.float32), 0.5, 1.5)
    w_query = gaussian(arg_keys[8], (D, D), D ** -0.5, 0.1875, ((1, 4),))
    w_key = gaussian(arg_keys[9], (D, D), D ** -0.5, 0.1875, ((1, 4),))
    w_value = gaussian(arg_keys[10], (D, D), D ** -0.5, 0.1875, ((1, 4),))
    w_out = gaussian(arg_keys[11], (D, D), D ** -0.5, 0.1875, ((0, 4),))
    return {"events": events, "event_owner": event_owner, "event_user": event_user, "cache_keys": cache_keys, "cache_values": cache_values, "cache_len": cache_len, "user_rank": user_rank, "norm_gain": norm_gain, "w_query": w_query, "w_key": w_key, "w_value": w_value, "w_out": w_out}


def attend(query, keys, values, allowed, head_dim):
    rows = query.shape[0]
    count = keys.shape[0]
    nheads = query.shape[1] // head_dim
    qheads = query.reshape(rows, nheads, head_dim).transpose(1, 0, 2)
    kheads = keys.reshape(count, nheads, head_dim).transpose(1, 0, 2)
    vheads = values.reshape(count, nheads, head_dim).transpose(1, 0, 2)

    def single(pieces):
        qpart, kpart, vpart = pieces
        scores = jnp.dot(qpart, kpart.T, preferred_element_type=jnp.float32) * head_dim ** (-0.5)
        scores = jnp.where(allowed, scores, -jnp.inf)
        top = lax.optimization_barrier(jnp.max(scores, axis=1, keepdims=True))
        weights = jnp.exp(scores - top)
        probs = (weights / lax.optimization_barrier(jnp.sum(weights, axis=1, keepdims=True))).astype(jnp.bfloat16)
        return jnp.dot(probs, vpart, preferred_element_type=jnp.float32).astype(jnp.bfloat16)
    outcome = lax.map(single, (qheads, kheads, vheads))
    return outcome.transpose(1, 0, 2).reshape(rows, nheads * head_dim)

def refresh(rows, slot_user, own_keys, own_values, own_len, norm_gain, w_query, w_key, w_value, w_out):
    slots = rows.shape[0]
    valid = slot_user >= 0
    users = jnp.maximum(slot_user, 0)
    wide = rows.astype(jnp.float32)
    normed = (wide * lax.rsqrt(lax.optimization_barrier(jnp.mean(wide * wide, axis=1, keepdims=True)) + 1e-05) * norm_gain).astype(jnp.bfloat16)
    query = jnp.dot(normed, w_query, preferred_element_type=jnp.float32).astype(jnp.bfloat16)
    key_new = jnp.dot(normed, w_key, preferred_element_type=jnp.float32).astype(jnp.bfloat16)
    value_new = jnp.dot(normed, w_value, preferred_element_type=jnp.float32).astype(jnp.bfloat16)
    nusers, depth, width = own_keys.shape
    keys = jnp.concatenate([own_keys.reshape(nusers * depth, width), key_new], axis=0)
    values = jnp.concatenate([own_values.reshape(nusers * depth, width), value_new], axis=0)
    cached = jnp.arange(nusers * depth, dtype=jnp.int32)
    cache_user = cached // depth
    cache_live = cached % depth < jnp.repeat(own_len, depth)
    cache_ok = (users[:, None] == cache_user[None, :]) & cache_live[None, :]
    order = jnp.arange(slots, dtype=jnp.int32)
    new_ok = (users[:, None] == users[None, :]) & valid[None, :] & (order[None, :] <= order[:, None])
    new_ok = new_ok | (order[:, None] == order[None, :])
    allowed = jnp.concatenate([cache_ok, new_ok], axis=1)
    attn = attend(query, keys, values, allowed, HEAD_DIM)
    mixed = jnp.dot(attn, w_out, preferred_element_type=jnp.float32)
    updated = jnp.where(valid[:, None], (wide + mixed).astype(jnp.bfloat16), jnp.zeros((), jnp.bfloat16))
    which = jnp.arange(nusers, dtype=jnp.int32)
    hits = valid[None, :] & (users[None, :] == which[:, None])
    last = lax.optimization_barrier(jnp.max(jnp.where(hits, order[None, :], -1), axis=1))
    picker = (order[None, :] == last[:, None]).astype(jnp.bfloat16)
    state = jnp.dot(picker, updated, preferred_element_type=jnp.float32).astype(jnp.bfloat16)
    return (updated, state)

def reference(events, event_owner, event_user, cache_keys, cache_values, cache_len, user_rank, norm_gain, w_query, w_key, w_value, w_out):
    slots = N_USERS * CAP
    owner = event_owner[:, 0]
    onehot = (owner[:, None] == jnp.arange(N_USERS, dtype=jnp.int32)[None, :]).astype(jnp.int32)
    onehot = onehot.reshape(N_USERS, EV_DEV, N_USERS)
    before = (lax.optimization_barrier(jnp.sum(jnp.cumsum(onehot, axis=1) * onehot, axis=2)) - 1).reshape(-1)
    source = jnp.arange(EVENTS, dtype=jnp.int32) // EV_DEV
    target = source * CAP + before

    def per_owner(index):
        place = jnp.where(owner == index, target, slots)
        rows = jnp.zeros((slots, D), jnp.bfloat16).at[place].set(events, mode='drop')
        slot_user = jnp.full((slots,), -1, jnp.int32).at[place].set(event_user, mode='drop')
        return refresh(rows, slot_user, cache_keys[index], cache_values[index], cache_len[index], norm_gain, w_query, w_key, w_value, w_out)
    refreshed, states = lax.map(per_owner, jnp.arange(N_USERS, dtype=jnp.int32))
    flat_states = states.reshape(N_USERS * U_DEV, D)
    flat_rank = user_rank.reshape(-1)

    def per_ranker(index):
        return jnp.where((flat_rank == index)[:, None], flat_states, jnp.zeros((), jnp.bfloat16))
    ranked = lax.map(per_ranker, jnp.arange(N_USERS, dtype=jnp.int32))
    return (refreshed, ranked)
```

```python
import functools

import jax
import jax.numpy as jnp
from jax import lax
from jax.experimental import pallas as pl
from jax.experimental.pallas import tpu as pltpu
from jax.sharding import PartitionSpec as P

HEAD_DIM = 64
LANES = 128
CHUNK = 10
BIG = 1e30
VMEM = 48 * 1024 * 1024


def iota(shape, axis):
    return lax.broadcasted_iota(jnp.int32, shape, axis)


def route_kernel(owners, cap, owner_ref, user_ref, events_ref, out_ref):
    owner = owner_ref[...]
    user = user_ref[...]
    count = owner.shape[1]
    member = (iota((owners, count), 0) == owner).astype(jnp.bfloat16)
    same = lax.dot_general(member, member, (((0,), (0,)), ((), ())), preferred_element_type=jnp.float32)
    earlier = iota((count, count), 0) < iota((count, count), 1)
    rank = jnp.sum(jnp.where(earlier, same, 0.0), axis=0, keepdims=True).astype(jnp.int32)
    target = owner * CHUNK + rank
    line = iota((owners * CHUNK, 1), 0)
    dest = jnp.floor((line.astype(jnp.float32) + 0.5) * (1.0 / CHUNK)).astype(jnp.int32)
    part = line - dest * CHUNK
    slot = jnp.where(part >= cap, part - cap, part)
    slot_line = jnp.where(part < 2 * cap, dest * CHUNK + slot, -1)
    user_line = jnp.where(part == 2 * cap, dest, -1)
    pick = jnp.where((slot_line == target) | (user_line == owner), 1.0, 0.0).astype(jnp.bfloat16)
    rows = jnp.dot(pick, events_ref[...], preferred_element_type=jnp.float32)
    named = jnp.where(iota((LANES, count), 0) == rank, user + 1, 0).astype(jnp.float32).astype(jnp.bfloat16)
    users = lax.dot_general(pick, named, (((1,), (1,)), ((), ())), preferred_element_type=jnp.float32) - 1.0
    value = jnp.where(part < cap, rows[:, :LANES], rows[:, LANES:])
    value = jnp.where(part < 2 * cap, value, jnp.where(part == 2 * cap, users, 0.0))
    out_ref[...] = value.astype(jnp.bfloat16)


def attend_kernel(
    rows_ref, meta_ref, len_ref, gain_ref, wq_ref, wk_ref, wv_ref, ck_ref, cv_ref, wo_ref,
    out_ref, normed_ref, query_ref, key_ref, value_ref, attn_ref,
):
    groups, parts, sources, _ = rows_ref.shape
    cap = parts // 2
    slots = cap * sources
    depth = ck_ref.shape[1]
    cached = 2 * depth
    for k in range(cap):
        wide = jnp.concatenate(
            [rows_ref[g, half * cap + k] for g in range(groups) for half in range(2)], axis=1
        ).astype(jnp.float32)
        mean = jnp.mean(wide * wide, axis=1, keepdims=True)
        normed = wide * lax.rsqrt(mean + 1e-05) * gain_ref[...]
        normed_ref[k * sources:(k + 1) * sources, :] = normed.astype(jnp.bfloat16)
    normed = normed_ref[...]
    query = jnp.dot(normed, wq_ref[...], preferred_element_type=jnp.float32).astype(jnp.bfloat16)
    query_ref[...] = query * jnp.bfloat16(HEAD_DIM ** -0.5)
    key_ref[...] = jnp.dot(normed, wk_ref[...], preferred_element_type=jnp.float32).astype(jnp.bfloat16)
    value_ref[...] = jnp.dot(normed, wv_ref[...], preferred_element_type=jnp.float32).astype(jnp.bfloat16)

    users = jnp.concatenate([meta_ref[:, k:k + 1] for k in range(cap)], axis=0).astype(jnp.float32)
    place = iota((cached, 1), 0)
    first = place < depth
    limit = jnp.where(first, len_ref[0, 0], len_ref[0, 1] + depth)
    cache_user = jnp.where(place < limit, jnp.where(first, 0.0, 1.0), -1.0)
    key_user = jnp.concatenate([cache_user, users], axis=0)
    lane = iota((1, LANES), 1)
    total = cached + slots
    row = iota((sources, sources), 0)
    col = iota((sources, sources), 1)
    upto = jnp.where(col <= row, 0.0, -BIG)
    under = jnp.where(col < row, 0.0, -BIG)
    for side in range(2):
        inside = lane // HEAD_DIM == side
        inside_one = jnp.where(inside, 1.0, 0.0).astype(jnp.bfloat16)
        outside_one = jnp.where(inside, 0.0, 1.0).astype(jnp.bfloat16)
        base = HEAD_DIM * (1 - side)
        wrong = jnp.where(lane == base, jnp.where(key_user == 0.0, 0.0, -BIG), 0.0)
        wrong = wrong + jnp.where(lane == base + 1, jnp.where(key_user == 1.0, 0.0, -BIG), 0.0)
        wrong = wrong.astype(jnp.bfloat16)
        asks = jnp.where(lane == base, jnp.where(users == 1.0, 0.0, 1.0), 0.0)
        asks = asks + jnp.where(lane == base + 1, jnp.where(users == 1.0, 1.0, 0.0), 0.0)
        asks = asks.astype(jnp.bfloat16)
        for pair in range(2):
            at = slice(pair * LANES, (pair + 1) * LANES)
            keys = jnp.concatenate([ck_ref[0, :, at], ck_ref[1, :, at], key_ref[:, at]], axis=0)
            keys = keys * inside_one + wrong
            values = jnp.concatenate([cv_ref[0, :, at], cv_ref[1, :, at], value_ref[:, at]], axis=0)
            values = values * inside_one + outside_one
            queries = query_ref[:, at] * inside_one + asks
            for k in range(cap):
                rows = slice(k * sources, (k + 1) * sources)
                scores = lax.dot_general(
                    queries[rows], keys, (((1,), (1,)), ((), ())), preferred_element_type=jnp.float32
                )
                bias = jnp.concatenate([upto if other <= k else under for other in range(cap)], axis=1)
                fresh = scores[:, cached:] + bias
                old = scores[:, :cached]
                top = jnp.maximum(jnp.max(old, axis=1, keepdims=True), jnp.max(fresh, axis=1, keepdims=True))
                weights = jnp.concatenate(
                    [jnp.exp(old - top).astype(jnp.bfloat16), jnp.exp(fresh - top).astype(jnp.bfloat16)], axis=1
                )
                mixed = jnp.dot(weights, values, preferred_element_type=jnp.float32)
                mixed = (mixed / pltpu.roll(mixed, HEAD_DIM, 1)).astype(jnp.bfloat16)
                here = slice(pair * LANES + side * HEAD_DIM, pair * LANES + (side + 1) * HEAD_DIM)
                attn_ref[rows, here] = mixed[:, side * HEAD_DIM:(side + 1) * HEAD_DIM]
    attn = attn_ref[...]
    width = out_ref.shape[2]
    for g in range(groups):
        out_ref[g] = jnp.dot(
            attn, wo_ref[:, g * width:(g + 1) * width], preferred_element_type=jnp.float32
        ).astype(jnp.bfloat16)


def state_kernel(owners, rank_ref, meta_ref, rows_ref, terms_ref, out_ref):
    groups, slots, width = terms_ref.shape
    sources = meta_ref.shape[0]
    cap = slots // sources
    source = iota((sources, 1), 0)
    lines = []
    for user in range(2):
        last = jnp.full((1, 1), -1, jnp.int32)
        for k in range(cap):
            hit = meta_ref[:, k:k + 1].astype(jnp.float32) == user
            best = jnp.max(jnp.where(hit, source * cap + k, -1), axis=0, keepdims=True)
            last = jnp.maximum(last, best)
        lines.append(last)
    lane = iota((1, sources), 1)
    which = iota((8, 1), 0)
    last = jnp.where(which == 0, lines[0], jnp.where(which == 1, lines[1], -1))
    mixed = jnp.zeros((8, width), jnp.float32)
    base = jnp.zeros((8, width), jnp.float32)
    for k in range(cap):
        pick = jnp.where(lane * cap + k == last, 1.0, 0.0).astype(jnp.bfloat16)
        for g in range(groups):
            mixed = mixed + jnp.dot(
                pick, terms_ref[g, k * sources:(k + 1) * sources, :], preferred_element_type=jnp.float32
            )
        own = jnp.concatenate([rows_ref[k], rows_ref[cap + k]], axis=1)
        base = base + jnp.dot(pick, own, preferred_element_type=jnp.float32)
    state = base + mixed
    line = iota((owners * 4, 1), 0)
    dest, part = line >> 2, line & 3
    value = jnp.zeros((owners * 4, LANES), jnp.float32)
    for user in range(2):
        for half in range(2):
            mine = (part == user * 2 + half) & (dest == rank_ref[0, user])
            value = jnp.where(mine, state[user:user + 1, half * LANES:(half + 1) * LANES], value)
    out_ref[...] = value.astype(jnp.bfloat16)


def call(kernel, out, args, scratch=(), smem=(), cost=None):
    specs = [pl.BlockSpec(memory_space=pltpu.SMEM if i in smem else pltpu.VMEM) for i in range(len(args))]
    return pl.pallas_call(
        kernel,
        out_shape=out,
        in_specs=specs,
        out_specs=pl.BlockSpec(memory_space=pltpu.VMEM),
        scratch_shapes=list(scratch),
        cost_estimate=cost,
        compiler_params=pltpu.CompilerParams(vmem_limit_bytes=VMEM),
    )(*args)


def local(
    events, event_owner, event_user, cache_keys, cache_values, cache_len, user_rank,
    norm_gain, w_query, w_key, w_value, w_out,
):
    count, width = events.shape
    owners = lax.axis_size("users")
    groups = lax.axis_size("heads")
    cap = 2 * count // owners
    slots = owners * cap
    bf16 = jnp.bfloat16
    sent = call(
        functools.partial(route_kernel, owners, cap),
        jax.ShapeDtypeStruct((owners * CHUNK, LANES), bf16),
        (event_owner.reshape(1, count), event_user.reshape(1, count), events),
    )
    got = lax.all_to_all(
        sent.reshape(owners, CHUNK // 2, 2, LANES), "users", split_axis=0, concat_axis=0, tiled=True
    )
    got = got.reshape(owners, CHUNK, LANES).transpose(1, 0, 2)
    own, meta = got[:2 * cap], got[2 * cap]
    full = lax.all_to_all(
        jnp.broadcast_to(own, (groups,) + own.shape), "heads", split_axis=0, concat_axis=0, tiled=True
    )
    terms = call(
        attend_kernel,
        jax.ShapeDtypeStruct((groups, slots, width), bf16),
        (
            full, meta, cache_len, norm_gain.reshape(1, -1), w_query, w_key, w_value,
            cache_keys[0], cache_values[0], w_out,
        ),
        scratch=[
            pltpu.VMEM((slots, groups * width), bf16),
            pltpu.VMEM((slots, width), bf16),
            pltpu.VMEM((slots, width), bf16),
            pltpu.VMEM((slots, width), bf16),
            pltpu.VMEM((slots, width), bf16),
        ],
        smem=(2,),
    )
    terms = lax.all_to_all(terms, "heads", split_axis=0, concat_axis=0, tiled=True)
    outgoing = call(
        functools.partial(state_kernel, owners),
        jax.ShapeDtypeStruct((owners * 4, LANES), bf16),
        (user_rank, meta, own, terms),
        smem=(0,),
    )
    arrived = lax.all_to_all(
        outgoing.reshape(owners, 4, LANES), "users", split_axis=0, concat_axis=0, tiled=True
    )
    ranked = arrived.reshape(1, owners * 2, width)

    mixed = jnp.sum(terms.astype(jnp.float32), axis=0).reshape(cap, owners, width)
    base = own.reshape(2, cap, owners, LANES).transpose(1, 2, 0, 3).reshape(cap, owners, width)
    valid = meta[:, :cap].T >= 0
    updated = jnp.where(valid[:, :, None], (base.astype(jnp.float32) + mixed).astype(bf16), jnp.zeros((), bf16))
    refreshed = updated.transpose(1, 0, 2).reshape(1, slots, width)
    return refreshed, ranked


def solution(mesh):
    placed = (
        P("users", "heads"),
        P("users", None),
        P("users"),
        P("users", None, None, "heads"),
        P("users", None, None, "heads"),
        P("users", None),
        P("users", None),
        P(),
        P(None, "heads"),
        P(None, "heads"),
        P(None, "heads"),
        P("heads", None),
    )
    return jax.shard_map(
        local,
        mesh=mesh,
        in_specs=placed,
        out_specs=(P("users", None, "heads"), P("users", None, "heads")),
        check_vma=False,
    )
```

```python
import functools

import jax
import jax.numpy as jnp
from jax import lax
from jax.experimental import pallas as pl
from jax.experimental.pallas import tpu as pltpu
from jax.sharding import PartitionSpec as P

HEAD_DIM = 64
LANES = 128
CHUNK = 10
BIG = 1e30
LAST_FLOPS = 30_000_000_000
STEP = 2
EDGE = 16
VMEM = 16 * 1024 * 1024


def iota(shape, axis):
    return lax.broadcasted_iota(jnp.int32, shape, axis)


def route_kernel(owners, cap, owner_hbm, user_hbm, events_hbm, out_ref, owner_ref, user_ref, events_ref, sems):
    copies = [
        pltpu.make_async_copy(source, target, sems.at[i])
        for i, (source, target) in enumerate(
            [(owner_hbm, owner_ref), (user_hbm, user_ref), (events_hbm, events_ref)]
        )
    ]
    for copy in copies:
        copy.start()
    copies[0].wait()
    copies[1].wait()
    owner = owner_ref[...]
    user = user_ref[...]
    count = owner.shape[1]
    member = (iota((owners, count), 0) == owner).astype(jnp.bfloat16)
    same = lax.dot_general(member, member, (((0,), (0,)), ((), ())), preferred_element_type=jnp.float32)
    earlier = iota((count, count), 0) < iota((count, count), 1)
    rank = jnp.sum(jnp.where(earlier, same, 0.0), axis=0, keepdims=True).astype(jnp.int32)
    target = owner * CHUNK + rank
    line = iota((owners * CHUNK, 1), 0)
    dest = jnp.floor((line.astype(jnp.float32) + 0.5) * (1.0 / CHUNK)).astype(jnp.int32)
    part = line - dest * CHUNK
    slot = jnp.where(part >= cap, part - cap, part)
    slot_line = jnp.where(part < 2 * cap, dest * CHUNK + slot, -1)
    user_line = jnp.where(part == 2 * cap, dest, -1)
    pick = jnp.where((slot_line == target) | (user_line == owner), 1.0, 0.0).astype(jnp.bfloat16)
    copies[2].wait()
    rows = jnp.dot(pick, events_ref[...], preferred_element_type=jnp.float32)
    named = jnp.where(iota((LANES, count), 0) == rank, user + 1, 0).astype(jnp.float32).astype(jnp.bfloat16)
    users = lax.dot_general(pick, named, (((1,), (1,)), ((), ())), preferred_element_type=jnp.float32) - 1.0
    value = jnp.where(part < cap, rows[:, :LANES], rows[:, LANES:])
    value = jnp.where(part < 2 * cap, value, jnp.where(part == 2 * cap, users, 0.0))
    out_ref[...] = value.astype(jnp.bfloat16)


def attend_kernel(
    rows_ref, got_ref, len_ref, gain_ref, wq_ref, wk_ref, wv_ref, ck_ref, cv_ref, wo_ref,
    own_ref, next_ref, across_ref, prev_ref, edge_ref, base_ref, normed_ref, query_ref, key_ref, value_ref, attn_ref,
):
    groups, parts, sources, _ = rows_ref.shape
    cap = parts // 2
    slots = cap * sources
    depth = ck_ref.shape[1]
    for k in range(cap):
        wide = jnp.concatenate(
            [rows_ref[g, half * cap + k] for g in range(groups) for half in range(2)], axis=1
        ).astype(jnp.float32)
        mean = jnp.mean(wide * wide, axis=1, keepdims=True)
        normed = wide * lax.rsqrt(mean + 1e-05) * gain_ref[...]
        normed_ref[k * sources:(k + 1) * sources, :] = normed.astype(jnp.bfloat16)
    normed = normed_ref[...]
    query = jnp.dot(normed, wq_ref[...], preferred_element_type=jnp.float32).astype(jnp.bfloat16)
    query_ref[...] = query * jnp.bfloat16(HEAD_DIM ** -0.5)
    key_ref[...] = jnp.dot(normed, wk_ref[...], preferred_element_type=jnp.float32).astype(jnp.bfloat16)
    value_ref[...] = jnp.dot(normed, wv_ref[...], preferred_element_type=jnp.float32).astype(jnp.bfloat16)

    meta = got_ref[2 * cap].astype(jnp.float32)
    users = jnp.concatenate([meta[:, k:k + 1] for k in range(cap)], axis=0)
    second = jnp.where(users == 1.0, 1.0, 0.0)
    lane = iota((1, LANES), 1)
    low = lane < HEAD_DIM
    low_one = jnp.where(low, 1.0, 0.0).astype(jnp.bfloat16)
    high_one = jnp.where(low, 0.0, 1.0).astype(jnp.bfloat16)
    asks = jnp.where(lane == 0, 1.0 - second, jnp.where(lane == 1, second, 0.0)).astype(jnp.bfloat16)
    place = iota((depth, 1), 0)
    wrong_old = jnp.where(
        lane == 0,
        jnp.where(place < len_ref[0, 0], 0.0, -BIG),
        jnp.where(lane == 1, jnp.where(place < len_ref[0, 1], 0.0, -BIG), 0.0),
    )
    wrong_new = jnp.where(
        lane == 0,
        jnp.where(users == 0.0, 0.0, -BIG),
        jnp.where(lane == 1, jnp.where(users == 1.0, 0.0, -BIG), 0.0),
    )
    wrong = jnp.concatenate([wrong_old, wrong_new], axis=0).astype(jnp.bfloat16)
    ones = jnp.ones((depth + slots, LANES), jnp.bfloat16)
    row = iota((sources, sources), 0)
    col = iota((sources, sources), 1)
    upto = jnp.where(col <= row, 0.0, -BIG)
    under = jnp.where(col < row, 0.0, -BIG)
    for pair in range(2):
        at = slice(pair * LANES, (pair + 1) * LANES)
        q, k_new, v_new = query_ref[:, at], key_ref[:, at], value_ref[:, at]
        k_one, v_one = ck_ref[0, :, at], cv_ref[0, :, at]
        q_turn, k_turn, v_turn = (pltpu.roll(x, HEAD_DIM, 1) for x in (q, k_new, v_new))
        k_two, v_two = pltpu.roll(ck_ref[1, :, at], HEAD_DIM, 1), pltpu.roll(cv_ref[1, :, at], HEAD_DIM, 1)
        for side in range(2):
            mine, other = (low_one, high_one) if side == 0 else (high_one, low_one)
            in_mine, in_other = (low, ~low) if side == 0 else (~low, low)
            held = jnp.where(in_mine, 1.0 - second, second).astype(jnp.bfloat16)
            queries = jnp.concatenate([(q * mine + q_turn * other) * held, asks], axis=1)
            keys = jnp.concatenate([k_one * mine + k_two * other, k_new * mine + k_turn * other], axis=0)
            keys = jnp.concatenate([keys, wrong], axis=1)
            values = jnp.concatenate([v_one * mine + v_two * other, v_new * mine + v_turn * other], axis=0)
            values = jnp.concatenate([values, ones], axis=1)
            for t in range(0, cap, STEP):
                rows = slice(t * sources, (t + STEP) * sources)
                scores = lax.dot_general(
                    queries[rows], keys, (((1,), (1,)), ((), ())), preferred_element_type=jnp.float32
                )
                bias = jnp.concatenate(
                    [
                        jnp.concatenate([upto if o <= k else under for o in range(cap)], axis=1)
                        for k in range(t, t + STEP)
                    ],
                    axis=0,
                )
                old, fresh = scores[:, :depth], scores[:, depth:] + bias
                top = jnp.maximum(jnp.max(old, axis=1, keepdims=True), jnp.max(fresh, axis=1, keepdims=True))
                weights = jnp.concatenate(
                    [jnp.exp(old - top).astype(jnp.bfloat16), jnp.exp(fresh - top).astype(jnp.bfloat16)], axis=1
                )
                mixed = jnp.dot(weights, values, preferred_element_type=jnp.float32)
                mixed, total = mixed[:, :LANES], mixed[:, LANES:]
                turned = pltpu.roll(mixed, HEAD_DIM, 1)
                mixed = jnp.where(second[rows] == 1.0, turned, mixed) / total
                here = slice(pair * LANES + side * HEAD_DIM, pair * LANES + (side + 1) * HEAD_DIM)
                attn_ref[rows, here] = mixed[:, side * HEAD_DIM:(side + 1) * HEAD_DIM].astype(jnp.bfloat16)
    attn = attn_ref[...]
    width = own_ref.shape[1]
    source = iota((sources, 1), 0)
    lane_source = iota((1, sources), 1)
    which = iota((EDGE, 1), 0)
    last = jnp.full((EDGE, 1), -1, jnp.int32)
    for user in range(2):
        for k in range(cap):
            hit = jnp.where(meta[:, k:k + 1] == user, source * cap + k, -1)
            best = jnp.max(hit, axis=0, keepdims=True)
            last = jnp.where(which == user, jnp.maximum(last, best), last)
    picks = [
        jnp.where(lane_source * cap + k == last, 1.0, 0.0).astype(jnp.bfloat16) for k in range(cap)
    ]
    base = jnp.zeros((EDGE, width), jnp.float32)
    for k in range(cap):
        own = jnp.concatenate([got_ref[k], got_ref[cap + k]], axis=1)
        base = base + jnp.dot(picks[k], own, preferred_element_type=jnp.float32)
    base_ref[...] = base
    final = jnp.dot(jnp.concatenate(picks, axis=1), attn, preferred_element_type=jnp.float32).astype(jnp.bfloat16)
    me = lax.axis_index("heads")
    for shift, out_ref in enumerate((own_ref, next_ref, across_ref, prev_ref)):
        group = lax.rem(me + shift, groups)
        part = wo_ref[:, pl.ds(pl.multiple_of(group * width, width), width)]
        out_ref[...] = jnp.dot(attn, part, preferred_element_type=jnp.float32).astype(jnp.bfloat16)
        edge_ref[group] = jnp.dot(final, part, preferred_element_type=jnp.float32).astype(jnp.bfloat16)


def state_kernel(owners, rank_ref, base_ref, terms_ref, out_ref):
    state = base_ref[...]
    for g in range(terms_ref.shape[0]):
        state = state + terms_ref[g].astype(jnp.float32)
    line = iota((owners * 4, 1), 0)
    dest, part = line >> 2, line & 3
    value = jnp.zeros((owners * 4, LANES), jnp.float32)
    for user in range(2):
        for half in range(2):
            mine = (part == user * 2 + half) & (dest == rank_ref[0, user])
            value = jnp.where(mine, state[user:user + 1, half * LANES:(half + 1) * LANES], value)
    out_ref[...] = value.astype(jnp.bfloat16)


def ranked_kernel(arrived_ref, out_ref):
    count = out_ref.shape[0]
    line = iota((1, 2 * count), 1)
    row = iota((count, 1), 0)
    for half in range(2):
        pick = jnp.where(line == 2 * row + half, 1.0, 0.0).astype(jnp.bfloat16)
        out_ref[:, half * LANES:(half + 1) * LANES] = jnp.dot(
            pick, arrived_ref[...], preferred_element_type=jnp.float32
        ).astype(jnp.bfloat16)


def refresh_kernel(got_ref, *refs):
    *term_refs, out_ref = refs
    slots, width = out_ref.shape
    _, sources, _ = got_ref.shape
    cap = slots // sources
    meta = got_ref[2 * cap].astype(jnp.float32)
    parts = []
    for k in range(cap):
        rows = slice(k * sources, (k + 1) * sources)
        mixed = sum(ref[rows, :].astype(jnp.float32) for ref in term_refs)
        own = jnp.concatenate([got_ref[k], got_ref[cap + k]], axis=1).astype(jnp.float32)
        parts.append(jnp.where(meta[:, k:k + 1] >= 0.0, own + mixed, 0.0).astype(jnp.bfloat16))
    updated = jnp.concatenate(parts, axis=0)
    line = iota((1, slots), 1)
    row = iota((slots, 1), 0)
    pick = jnp.where((line & (sources - 1)) * cap + line // sources == row, 1.0, 0.0).astype(jnp.bfloat16)
    out_ref[...] = jnp.dot(pick, updated, preferred_element_type=jnp.float32).astype(jnp.bfloat16)


def call(kernel, out, args, scratch=(), smem=(), hbm=(), cost=None, vmem=VMEM):
    specs = [
        pl.BlockSpec(memory_space=pltpu.SMEM if i in smem else pltpu.HBM if i in hbm else pltpu.VMEM)
        for i in range(len(args))
    ]
    return pl.pallas_call(
        kernel,
        out_shape=out,
        in_specs=specs,
        out_specs=jax.tree.map(lambda _: pl.BlockSpec(memory_space=pltpu.VMEM), out),
        scratch_shapes=list(scratch),
        cost_estimate=cost,
        compiler_params=pltpu.CompilerParams(vmem_limit_bytes=vmem),
    )(*args)


def local(
    events, event_owner, event_user, cache_keys, cache_values, cache_len, user_rank,
    norm_gain, w_query, w_key, w_value, w_out,
):
    count, width = events.shape
    owners = lax.axis_size("users")
    groups = lax.axis_size("heads")
    cap = 2 * count // owners
    slots = owners * cap
    bf16 = jnp.bfloat16
    sent = call(
        functools.partial(route_kernel, owners, cap),
        jax.ShapeDtypeStruct((owners * CHUNK, LANES), bf16),
        (event_owner.reshape(1, count), event_user.reshape(1, count), events),
        scratch=[
            pltpu.VMEM((1, count), jnp.int32),
            pltpu.VMEM((1, count), jnp.int32),
            pltpu.VMEM((count, width), bf16),
            pltpu.SemaphoreType.DMA((3,)),
        ],
        hbm=(0, 1, 2),
        vmem=60 * 1024 * 1024,
    )
    got = lax.all_to_all(
        sent.reshape(owners, CHUNK // 2, 2, LANES), "users", split_axis=0, concat_axis=0, tiled=True
    )
    got = got.reshape(owners, CHUNK, LANES).transpose(1, 0, 2)
    own = got[:2 * cap]
    full = lax.all_to_all(
        jnp.broadcast_to(own, (groups,) + own.shape), "heads", split_axis=0, concat_axis=0, tiled=True
    )
    got, full = lax.optimization_barrier((got, full))
    own = got[:2 * cap]
    *terms, edge, base = call(
        attend_kernel,
        (jax.ShapeDtypeStruct((slots, width), bf16),) * groups
        + (
            jax.ShapeDtypeStruct((groups, EDGE, width), bf16),
            jax.ShapeDtypeStruct((EDGE, width), jnp.float32),
        ),
        (
            full, got, cache_len, norm_gain.reshape(1, -1), w_query, w_key, w_value,
            cache_keys[0], cache_values[0], w_out,
        ),
        scratch=[
            pltpu.VMEM((slots, groups * width), bf16),
            pltpu.VMEM((slots, width), bf16),
            pltpu.VMEM((slots, width), bf16),
            pltpu.VMEM((slots, width), bf16),
            pltpu.VMEM((slots, width), bf16),
        ],
        smem=(2,),
    )
    edge = lax.all_to_all(edge, "heads", split_axis=0, concat_axis=0, tiled=True)
    outgoing = call(
        functools.partial(state_kernel, owners),
        jax.ShapeDtypeStruct((owners * 4, LANES), bf16),
        (user_rank, base, edge),
        smem=(0,),
    )
    outgoing, terms = lax.optimization_barrier((outgoing, terms))
    terms = [terms[0]] + [
        lax.ppermute(terms[shift], "heads", [(g, (g + shift) % groups) for g in range(groups)])
        for shift in range(1, groups)
    ]
    arrived = lax.all_to_all(
        outgoing.reshape(owners, 4, LANES), "users", split_axis=0, concat_axis=0, tiled=True
    )
    ranked = call(
        ranked_kernel,
        jax.ShapeDtypeStruct((owners * 2, width), bf16),
        (arrived.reshape(owners * 4, LANES),),
        cost=pl.CostEstimate(flops=LAST_FLOPS, bytes_accessed=1 << 20, transcendentals=0),
    )
    refreshed = call(
        refresh_kernel,
        jax.ShapeDtypeStruct((slots, width), bf16),
        (got, *terms),
        cost=pl.CostEstimate(flops=300_000_000, bytes_accessed=1 << 20, transcendentals=0),
    )
    return refreshed[None], ranked[None]


def solution(mesh):
    placed = (
        P("users", "heads"),
        P("users", None),
        P("users"),
        P("users", None, None, "heads"),
        P("users", None, None, "heads"),
        P("users", None),
        P("users", None),
        P(),
        P(None, "heads"),
        P(None, "heads"),
        P(None, "heads"),
        P("heads", None),
    )
    return jax.shard_map(
        local,
        mesh=mesh,
        in_specs=placed,
        out_specs=(P("users", None, "heads"), P("users", None, "heads")),
        check_vma=False,
    )
```

```python
import functools

import jax
import jax.numpy as jnp
from jax import lax
from jax.experimental import pallas as pl
from jax.experimental.pallas import tpu as pltpu
from jax.sharding import PartitionSpec as P

HEAD_DIM = 64
LANES = 128
CHUNK = 10
BIG = 1e30
PICK_FLOPS = 30_000_000_000
STEP = 2
EDGE = 16
VMEM = 16 * 1024 * 1024


def iota(shape, axis):
    return lax.broadcasted_iota(jnp.int32, shape, axis)


def route_kernel(
    owners, cap, owner_hbm, user_hbm, events_hbm, gain_hbm, len_hbm, rank_hbm,
    out_ref, aux_ref, owner_ref, user_ref, events_ref, gain_ref, len_ref, rank_ref, sems,
):
    copies = [
        pltpu.make_async_copy(source, target, sems.at[i])
        for i, (source, target) in enumerate(
            [
                (owner_hbm, owner_ref), (user_hbm, user_ref), (events_hbm, events_ref),
                (gain_hbm, gain_ref), (len_hbm, len_ref), (rank_hbm, rank_ref),
            ]
        )
    ]
    for copy in copies:
        copy.start()
    copies[0].wait()
    copies[1].wait()
    owner = owner_ref[...]
    user = user_ref[...]
    count = owner.shape[1]
    member = (iota((owners, count), 0) == owner).astype(jnp.bfloat16)
    same = lax.dot_general(member, member, (((0,), (0,)), ((), ())), preferred_element_type=jnp.float32)
    earlier = iota((count, count), 0) < iota((count, count), 1)
    rank = jnp.sum(jnp.where(earlier, same, 0.0), axis=0, keepdims=True).astype(jnp.int32)
    target = owner * CHUNK + rank
    line = iota((owners * CHUNK, 1), 0)
    dest = jnp.floor((line.astype(jnp.float32) + 0.5) * (1.0 / CHUNK)).astype(jnp.int32)
    part = line - dest * CHUNK
    slot = jnp.where(part >= cap, part - cap, part)
    slot_line = jnp.where(part < 2 * cap, dest * CHUNK + slot, -1)
    user_line = jnp.where(part == 2 * cap, dest, -1)
    pick = jnp.where((slot_line == target) | (user_line == owner), 1.0, 0.0).astype(jnp.bfloat16)
    copies[2].wait()
    rows = jnp.dot(pick, events_ref[...], preferred_element_type=jnp.float32)
    named = jnp.where(iota((LANES, count), 0) == rank, user + 1, 0).astype(jnp.float32).astype(jnp.bfloat16)
    users = lax.dot_general(pick, named, (((1,), (1,)), ((), ())), preferred_element_type=jnp.float32) - 1.0
    value = jnp.where(part < cap, rows[:, :LANES], rows[:, LANES:])
    value = jnp.where(part < 2 * cap, value, jnp.where(part == 2 * cap, users, 0.0))
    out_ref[...] = value.astype(jnp.bfloat16)
    for copy in copies[3:]:
        copy.wait()
    wide = gain_ref.shape[1]
    lane = iota((1, LANES), 1)
    tail = jnp.where(lane == 0, len_ref[:, 0:1], jnp.where(lane == 1, len_ref[:, 1:2], 0))
    tail = jnp.where(lane == 2, rank_ref[:, 0:1], jnp.where(lane == 3, rank_ref[:, 1:2], tail))
    aux_ref[:, :wide] = gain_ref[...]
    aux_ref[:, wide:] = tail.astype(jnp.float32)


def attend_kernel(
    rows_ref, got_ref, aux_ref, wq_ref, wk_ref, wv_ref, ck_ref, cv_ref, wo_ref,
    own_ref, next_ref, across_ref, prev_ref, edge_ref, base_ref, normed_ref, query_ref, key_ref, value_ref, attn_ref,
):
    groups, parts, sources, _ = rows_ref.shape
    width = own_ref.shape[1]
    tail = aux_ref[:, groups * width:]
    cap = parts // 2
    slots = cap * sources
    depth = ck_ref.shape[1]
    for k in range(cap):
        wide = jnp.concatenate(
            [rows_ref[g, half * cap + k] for g in range(groups) for half in range(2)], axis=1
        ).astype(jnp.float32)
        mean = jnp.mean(wide * wide, axis=1, keepdims=True)
        normed = wide * lax.rsqrt(mean + 1e-05) * aux_ref[:, :groups * width]
        normed_ref[k * sources:(k + 1) * sources, :] = normed.astype(jnp.bfloat16)
    normed = normed_ref[...]
    query = jnp.dot(normed, wq_ref[...], preferred_element_type=jnp.float32).astype(jnp.bfloat16)
    query_ref[...] = query * jnp.bfloat16(HEAD_DIM ** -0.5)
    key_ref[...] = jnp.dot(normed, wk_ref[...], preferred_element_type=jnp.float32).astype(jnp.bfloat16)
    value_ref[...] = jnp.dot(normed, wv_ref[...], preferred_element_type=jnp.float32).astype(jnp.bfloat16)

    meta = got_ref[2 * cap].astype(jnp.float32)
    users = jnp.concatenate([meta[:, k:k + 1] for k in range(cap)], axis=0)
    second = jnp.where(users == 1.0, 1.0, 0.0)
    lane = iota((1, LANES), 1)
    low = lane < HEAD_DIM
    low_one = jnp.where(low, 1.0, 0.0).astype(jnp.bfloat16)
    high_one = jnp.where(low, 0.0, 1.0).astype(jnp.bfloat16)
    asks = jnp.where(lane == 0, 1.0 - second, jnp.where(lane == 1, second, 0.0)).astype(jnp.bfloat16)
    place = iota((depth, 1), 0).astype(jnp.float32)
    wrong_old = jnp.where(
        lane == 0,
        jnp.where(place < tail[:, 0:1], 0.0, -BIG),
        jnp.where(lane == 1, jnp.where(place < tail[:, 1:2], 0.0, -BIG), 0.0),
    )
    wrong_new = jnp.where(
        lane == 0,
        jnp.where(users == 0.0, 0.0, -BIG),
        jnp.where(lane == 1, jnp.where(users == 1.0, 0.0, -BIG), 0.0),
    )
    wrong = jnp.concatenate([wrong_old, wrong_new], axis=0).astype(jnp.bfloat16)
    ones = jnp.ones((depth + slots, LANES), jnp.bfloat16)
    row = iota((sources, sources), 0)
    col = iota((sources, sources), 1)
    upto = jnp.where(col <= row, 0.0, -BIG)
    under = jnp.where(col < row, 0.0, -BIG)
    def operands(pair):
        at = slice(pair * LANES, (pair + 1) * LANES)
        q, k_new, v_new = query_ref[:, at], key_ref[:, at], value_ref[:, at]
        k_one, v_one = ck_ref[0, :, at], cv_ref[0, :, at]
        q_turn, k_turn, v_turn = (pltpu.roll(x, HEAD_DIM, 1) for x in (q, k_new, v_new))
        k_two, v_two = pltpu.roll(ck_ref[1, :, at], HEAD_DIM, 1), pltpu.roll(cv_ref[1, :, at], HEAD_DIM, 1)
        for side in range(2):
            mine, other = (low_one, high_one) if side == 0 else (high_one, low_one)
            in_mine = low if side == 0 else ~low
            held = jnp.where(in_mine, 1.0 - second, second).astype(jnp.bfloat16)
            queries = jnp.concatenate([(q * mine + q_turn * other) * held, asks], axis=1)
            keys = jnp.concatenate([k_one * mine + k_two * other, k_new * mine + k_turn * other], axis=0)
            keys = jnp.concatenate([keys, wrong], axis=1)
            values = jnp.concatenate([v_one * mine + v_two * other, v_new * mine + v_turn * other], axis=0)
            values = jnp.concatenate([values, ones], axis=1)
            yield queries, keys, values

    heads = [head for pair in range(2) for head in operands(pair)]
    steps = [(h, t) for h in range(len(heads)) for t in range(0, cap, STEP)]

    def score(step):
        h, t = step
        queries, keys, _ = heads[h]
        return lax.dot_general(
            queries[t * sources:(t + STEP) * sources], keys, (((1,), (1,)), ((), ())),
            preferred_element_type=jnp.float32,
        )

    ahead = score(steps[0])
    for at, (h, t) in enumerate(steps):
        scores = ahead
        if at + 1 < len(steps):
            ahead = score(steps[at + 1])
        rows = slice(t * sources, (t + STEP) * sources)
        bias = jnp.concatenate(
            [
                jnp.concatenate([upto if o <= k else under for o in range(cap)], axis=1)
                for k in range(t, t + STEP)
            ],
            axis=0,
        )
        old, fresh = scores[:, :depth], scores[:, depth:] + bias
        top = jnp.maximum(jnp.max(old, axis=1, keepdims=True), jnp.max(fresh, axis=1, keepdims=True))
        weights = jnp.concatenate(
            [jnp.exp(old - top).astype(jnp.bfloat16), jnp.exp(fresh - top).astype(jnp.bfloat16)], axis=1
        )
        mixed = jnp.dot(weights, heads[h][2], preferred_element_type=jnp.float32)
        mixed, total = mixed[:, :LANES], mixed[:, LANES:]
        turned = pltpu.roll(mixed, HEAD_DIM, 1)
        mixed = jnp.where(second[rows] == 1.0, turned, mixed) / total
        side = h % 2
        attn_ref[rows, h * HEAD_DIM:(h + 1) * HEAD_DIM] = mixed[
            :, side * HEAD_DIM:(side + 1) * HEAD_DIM
        ].astype(jnp.bfloat16)
    attn = attn_ref[...]
    source = iota((sources, 1), 0)
    lane_source = iota((1, sources), 1)
    which = iota((EDGE, 1), 0)
    last = jnp.full((EDGE, 1), -1, jnp.int32)
    for user in range(2):
        for k in range(cap):
            hit = jnp.where(meta[:, k:k + 1] == user, source * cap + k, -1)
            best = jnp.max(hit, axis=0, keepdims=True)
            last = jnp.where(which == user, jnp.maximum(last, best), last)
    picks = [
        jnp.where(lane_source * cap + k == last, 1.0, 0.0).astype(jnp.bfloat16) for k in range(cap)
    ]
    base = jnp.zeros((EDGE, width), jnp.float32)
    for k in range(cap):
        own = jnp.concatenate([got_ref[k], got_ref[cap + k]], axis=1)
        base = base + jnp.dot(picks[k], own, preferred_element_type=jnp.float32)
    base_ref[:EDGE] = base
    base_ref[EDGE:, :LANES] = jnp.broadcast_to(tail, (8, LANES))
    base_ref[EDGE:, LANES:] = jnp.zeros((8, width - LANES), jnp.float32)
    final = jnp.dot(jnp.concatenate(picks, axis=1), attn, preferred_element_type=jnp.float32).astype(jnp.bfloat16)
    me = lax.axis_index("heads")
    for shift, out_ref in enumerate((own_ref, next_ref, across_ref, prev_ref)):
        group = lax.rem(me + shift, groups)
        part = wo_ref[:, pl.ds(pl.multiple_of(group * width, width), width)]
        out_ref[...] = jnp.dot(attn, part, preferred_element_type=jnp.float32).astype(jnp.bfloat16)
        edge_ref[group] = jnp.dot(final, part, preferred_element_type=jnp.float32).astype(jnp.bfloat16)


def state_kernel(owners, base_ref, terms_ref, out_ref):
    state = base_ref[:EDGE]
    ranks = base_ref[EDGE:EDGE + 1, :LANES].astype(jnp.int32)
    for g in range(terms_ref.shape[0]):
        state = state + terms_ref[g].astype(jnp.float32)
    line = iota((owners * 4, 1), 0)
    dest, part = line >> 2, line & 3
    value = jnp.zeros((owners * 4, LANES), jnp.float32)
    for user in range(2):
        for half in range(2):
            mine = (part == user * 2 + half) & (dest == ranks[:, 2 + user:3 + user])
            value = jnp.where(mine, state[user:user + 1, half * LANES:(half + 1) * LANES], value)
    out_ref[...] = value.astype(jnp.bfloat16)


def ranked_kernel(arrived_ref, out_ref):
    count = out_ref.shape[0]
    line = iota((1, 2 * count), 1)
    row = iota((count, 1), 0)
    for half in range(2):
        pick = jnp.where(line == 2 * row + half, 1.0, 0.0).astype(jnp.bfloat16)
        out_ref[:, half * LANES:(half + 1) * LANES] = jnp.dot(
            pick, arrived_ref[...], preferred_element_type=jnp.float32
        ).astype(jnp.bfloat16)


def refresh_kernel(got_ref, *refs):
    *term_refs, out_ref = refs
    slots, width = out_ref.shape
    _, sources, _ = got_ref.shape
    cap = slots // sources
    meta = got_ref[2 * cap].astype(jnp.float32)
    parts = []
    for k in range(cap):
        rows = slice(k * sources, (k + 1) * sources)
        mixed = sum(ref[rows, :].astype(jnp.float32) for ref in term_refs)
        own = jnp.concatenate([got_ref[k], got_ref[cap + k]], axis=1).astype(jnp.float32)
        parts.append(jnp.where(meta[:, k:k + 1] >= 0.0, own + mixed, 0.0).astype(jnp.bfloat16))
    updated = jnp.concatenate(parts, axis=0)
    line = iota((1, slots), 1)
    row = iota((slots, 1), 0)
    pick = jnp.where((line & (sources - 1)) * cap + line // sources == row, 1.0, 0.0).astype(jnp.bfloat16)
    out_ref[...] = jnp.dot(pick, updated, preferred_element_type=jnp.float32).astype(jnp.bfloat16)


def call(kernel, out, args, scratch=(), smem=(), hbm=(), cost=None, vmem=VMEM):
    specs = [
        pl.BlockSpec(memory_space=pltpu.SMEM if i in smem else pltpu.HBM if i in hbm else pltpu.VMEM)
        for i in range(len(args))
    ]
    return pl.pallas_call(
        kernel,
        out_shape=out,
        in_specs=specs,
        out_specs=jax.tree.map(lambda _: pl.BlockSpec(memory_space=pltpu.VMEM), out),
        scratch_shapes=list(scratch),
        cost_estimate=cost,
        compiler_params=pltpu.CompilerParams(vmem_limit_bytes=vmem),
    )(*args)


def local(
    events, event_owner, event_user, cache_keys, cache_values, cache_len, user_rank,
    norm_gain, w_query, w_key, w_value, w_out,
):
    count, width = events.shape
    owners = lax.axis_size("users")
    groups = lax.axis_size("heads")
    cap = 2 * count // owners
    slots = owners * cap
    bf16 = jnp.bfloat16
    wide = groups * width
    sent, aux = call(
        functools.partial(route_kernel, owners, cap),
        (
            jax.ShapeDtypeStruct((owners * CHUNK, LANES), bf16),
            jax.ShapeDtypeStruct((1, wide + LANES), jnp.float32),
        ),
        (
            event_owner.reshape(1, count), event_user.reshape(1, count), events,
            norm_gain.reshape(1, wide), cache_len, user_rank,
        ),
        scratch=[
            pltpu.VMEM((1, count), jnp.int32),
            pltpu.VMEM((1, count), jnp.int32),
            pltpu.VMEM((count, width), bf16),
            pltpu.VMEM((1, wide), jnp.float32),
            pltpu.VMEM((1, 2), jnp.int32),
            pltpu.VMEM((1, 2), jnp.int32),
            pltpu.SemaphoreType.DMA((6,)),
        ],
        hbm=(0, 1, 2, 3, 4, 5),
        vmem=60 * 1024 * 1024,
    )
    got = lax.all_to_all(
        sent.reshape(owners, CHUNK // 2, 2, LANES), "users", split_axis=0, concat_axis=0, tiled=True
    )
    got = got.reshape(owners, CHUNK, LANES).transpose(1, 0, 2)
    own = got[:2 * cap]
    full = lax.all_to_all(
        jnp.broadcast_to(own, (groups,) + own.shape), "heads", split_axis=0, concat_axis=0, tiled=True
    )
    got, full = lax.optimization_barrier((got, full))
    own = got[:2 * cap]
    *terms, edge, base = call(
        attend_kernel,
        (jax.ShapeDtypeStruct((slots, width), bf16),) * groups
        + (
            jax.ShapeDtypeStruct((groups, EDGE, width), bf16),
            jax.ShapeDtypeStruct((EDGE + 8, width), jnp.float32),
        ),
        (
            full, got, aux, w_query, w_key, w_value,
            cache_keys[0], cache_values[0], w_out,
        ),
        scratch=[
            pltpu.VMEM((slots, groups * width), bf16),
            pltpu.VMEM((slots, width), bf16),
            pltpu.VMEM((slots, width), bf16),
            pltpu.VMEM((slots, width), bf16),
            pltpu.VMEM((slots, width), bf16),
        ],
    )
    edge = lax.all_to_all(edge, "heads", split_axis=0, concat_axis=0, tiled=True)
    outgoing = call(
        functools.partial(state_kernel, owners),
        jax.ShapeDtypeStruct((owners * 4, LANES), bf16),
        (base, edge),
        cost=pl.CostEstimate(flops=PICK_FLOPS, bytes_accessed=1 << 20, transcendentals=0),
    )
    def passed(term, shift):
        return lax.ppermute(term, "heads", [(g, (g + shift) % groups) for g in range(groups)])

    across = passed(terms[2], 2)
    outgoing, one, three = lax.optimization_barrier((outgoing, terms[1], terms[3]))
    terms = [terms[0], passed(one, 1), across, passed(three, 3)]
    arrived = lax.all_to_all(
        outgoing.reshape(owners, 4, LANES), "users", split_axis=0, concat_axis=0, tiled=True
    )
    arrived, across = lax.optimization_barrier((arrived, across))
    terms[2] = across
    ranked = call(
        ranked_kernel,
        jax.ShapeDtypeStruct((owners * 2, width), bf16),
        (arrived.reshape(owners * 4, LANES),),
        cost=pl.CostEstimate(flops=PICK_FLOPS, bytes_accessed=1 << 20, transcendentals=0),
    )
    refreshed = call(
        refresh_kernel,
        jax.ShapeDtypeStruct((slots, width), bf16),
        (got, *terms),
        cost=pl.CostEstimate(flops=300_000_000, bytes_accessed=1 << 20, transcendentals=0),
    )
    return refreshed[None], ranked[None]


def solution(mesh):
    placed = (
        P("users", "heads"),
        P("users", None),
        P("users"),
        P("users", None, None, "heads"),
        P("users", None, None, "heads"),
        P("users", None),
        P("users", None),
        P(),
        P(None, "heads"),
        P(None, "heads"),
        P(None, "heads"),
        P("heads", None),
    )
    return jax.shard_map(
        local,
        mesh=mesh,
        in_specs=placed,
        out_specs=(P("users", None, "heads"), P("users", None, "heads")),
        check_vma=False,
    )
```

```python
import functools

import jax
import jax.numpy as jnp
from jax import lax
from jax.experimental import pallas as pl
from jax.experimental.pallas import tpu as pltpu
from jax.sharding import PartitionSpec as P

HEAD_DIM = 64
LANES = 128
CHUNK = 10
BIG = 1e30
PICK_FLOPS = 30_000_000_000
STEP = 2
PIECES = 32
EDGE = 16
VMEM = 16 * 1024 * 1024


def iota(shape, axis):
    return lax.broadcasted_iota(jnp.int32, shape, axis)


def route_kernel(
    owners, cap, owner_hbm, user_hbm, events_hbm, gain_hbm, len_hbm, rank_hbm,
    out_hbm, made_ref, owner_ref, user_ref, events_ref, gain_ref, len_ref, rank_ref, sems,
):
    copies = [
        pltpu.make_async_copy(source, target, sems.at[i])
        for i, (source, target) in enumerate(
            [
                (owner_hbm, owner_ref), (user_hbm, user_ref), (events_hbm, events_ref),
                (gain_hbm, gain_ref), (len_hbm, len_ref), (rank_hbm, rank_ref),
            ]
        )
    ]
    for copy in copies:
        copy.start()
    line = iota((owners * CHUNK, 1), 0)
    dest = jnp.floor((line.astype(jnp.float32) + 0.5) * (1.0 / CHUNK)).astype(jnp.int32)
    part = line - dest * CHUNK
    slot = jnp.where(part >= cap, part - cap, part)
    slot_line = jnp.where(part < 2 * cap, dest * CHUNK + slot, -1)
    user_line = jnp.where(part == 2 * cap, dest, -1)
    copies[0].wait()
    copies[1].wait()
    owner = owner_ref[...]
    user = user_ref[...]
    count = owner.shape[1]
    member = (iota((owners, count), 0) == owner).astype(jnp.bfloat16)
    same = lax.dot_general(member, member, (((0,), (0,)), ((), ())), preferred_element_type=jnp.float32)
    earlier = iota((count, count), 0) < iota((count, count), 1)
    rank = jnp.sum(jnp.where(earlier, same, 0.0), axis=0, keepdims=True).astype(jnp.int32)
    target = owner * CHUNK + rank
    named = jnp.where(iota((LANES, count), 0) == rank, user + 1, 0).astype(jnp.float32).astype(jnp.bfloat16)
    for copy in copies[2:]:
        copy.wait()
    me = lax.axis_index("users")
    piece = lax.rem(me, PIECES)
    gain = gain_ref[:, pl.ds(pl.multiple_of(lax.rem(piece, PIECES // 4) * LANES, LANES), LANES)]
    coarse = gain.astype(jnp.bfloat16).astype(jnp.float32)
    middle = (gain - coarse).astype(jnp.bfloat16).astype(jnp.float32)
    level = piece // (PIECES // 4)
    spare = jnp.where(level == 0, coarse, jnp.where(level == 1, middle, gain - coarse - middle))
    spare = jnp.where(level == 3, 0.0, spare)
    lane = iota((1, LANES), 1)
    back = jnp.zeros((1, LANES), jnp.int32)
    for user_at in range(2):
        length = len_ref[:, user_at:user_at + 1]
        back = jnp.where(lane == 3 * user_at, length >> 4, back)
        back = jnp.where(lane == 3 * user_at + 1, length & 15, back)
        back = jnp.where(lane == 3 * user_at + 2, rank_ref[:, user_at:user_at + 1], back)
    back = back.astype(jnp.float32)
    events = events_ref[...]
    half_lines = owners * CHUNK // 2
    leaving = []
    for half in range(2):
        at = slice(half * half_lines, (half + 1) * half_lines)
        pick = jnp.where((slot_line[at] == target) | (user_line[at] == owner), 1.0, 0.0).astype(jnp.bfloat16)
        rows = jnp.dot(pick, events, preferred_element_type=jnp.float32)
        users = lax.dot_general(pick, named, (((1,), (1,)), ((), ())), preferred_element_type=jnp.float32) - 1.0
        value = jnp.where(part[at] < cap, rows[:, :LANES], rows[:, LANES:])
        value = jnp.where(part[at] < 2 * cap, value, users)
        value = jnp.where(part[at] > 2 * cap, jnp.where(dest[at] == me, back, spare), value)
        made_ref[at, :] = value.astype(jnp.bfloat16)
        leaving.append(pltpu.make_async_copy(made_ref.at[at], out_hbm.at[at], sems.at[len(copies) + half]))
        leaving[half].start()
    for copy in leaving:
        copy.wait()


def attend_kernel(
    rows_ref, got_ref, wq_ref, wk_ref, wv_ref, ck_ref, cv_ref, wo_ref,
    own_ref, next_ref, across_ref, prev_ref, edge_hbm, base_ref, normed_ref, query_ref, key_ref, value_ref, attn_ref,
    edge_ref, sem,
):
    groups, parts, sources, _ = rows_ref.shape
    width = own_ref.shape[1]
    me_user = lax.axis_index("users")
    block = me_user // PIECES
    beside = jnp.where(block % 2 == 0, block + 1, block - 1)
    spare = got_ref[parts + 1, pl.ds(pl.multiple_of(beside * PIECES, PIECES), PIECES), :].astype(jnp.float32)
    fourth = PIECES // 4
    gain = spare[:fourth] + spare[fourth:2 * fourth] + spare[2 * fourth:3 * fourth]
    gain = jnp.concatenate([gain[g:g + 1] for g in range(fourth)], axis=1)
    back = got_ref[parts + 1, pl.ds(pl.multiple_of(block * PIECES, PIECES), PIECES), :].astype(jnp.float32)
    back = jnp.where(iota((PIECES, 1), 0) == lax.rem(me_user, PIECES), back, 0.0)
    back = jnp.sum(back, axis=0, keepdims=True)
    lengths = [back[:, 3 * user:3 * user + 1] * 16.0 + back[:, 3 * user + 1:3 * user + 2] for user in range(2)]
    ranks = [back[:, 3 * user + 2:3 * user + 3] for user in range(2)]
    cap = parts // 2
    slots = cap * sources
    depth = ck_ref.shape[1]
    for k in range(cap):
        wide = jnp.concatenate(
            [rows_ref[g, half * cap + k] for g in range(groups) for half in range(2)], axis=1
        ).astype(jnp.float32)
        mean = jnp.mean(wide * wide, axis=1, keepdims=True)
        normed = wide * lax.rsqrt(mean + 1e-05) * gain
        normed_ref[k * sources:(k + 1) * sources, :] = normed.astype(jnp.bfloat16)
    normed = normed_ref[...]
    query = jnp.dot(normed, wq_ref[...], preferred_element_type=jnp.float32).astype(jnp.bfloat16)
    query_ref[...] = query * jnp.bfloat16(HEAD_DIM ** -0.5)
    key_ref[...] = jnp.dot(normed, wk_ref[...], preferred_element_type=jnp.float32).astype(jnp.bfloat16)
    value_ref[...] = jnp.dot(normed, wv_ref[...], preferred_element_type=jnp.float32).astype(jnp.bfloat16)

    meta = got_ref[2 * cap].astype(jnp.float32)
    users = jnp.concatenate([meta[:, k:k + 1] for k in range(cap)], axis=0)
    second = jnp.where(users == 1.0, 1.0, 0.0)
    lane = iota((1, LANES), 1)
    low = lane < HEAD_DIM
    low_one = jnp.where(low, 1.0, 0.0).astype(jnp.bfloat16)
    high_one = jnp.where(low, 0.0, 1.0).astype(jnp.bfloat16)
    asks = jnp.where(lane == 0, 1.0 - second, jnp.where(lane == 1, second, 0.0)).astype(jnp.bfloat16)
    place = iota((depth, 1), 0).astype(jnp.float32)
    wrong_old = jnp.where(
        lane == 0,
        jnp.where(place < lengths[0], 0.0, -BIG),
        jnp.where(lane == 1, jnp.where(place < lengths[1], 0.0, -BIG), 0.0),
    )
    wrong_new = jnp.where(
        lane == 0,
        jnp.where(users == 0.0, 0.0, -BIG),
        jnp.where(lane == 1, jnp.where(users == 1.0, 0.0, -BIG), 0.0),
    )
    wrong = jnp.concatenate([wrong_old, wrong_new], axis=0).astype(jnp.bfloat16)
    ones = jnp.ones((depth + slots, LANES), jnp.bfloat16)
    row = iota((sources, sources), 0)
    col = iota((sources, sources), 1)
    upto = jnp.where(col <= row, 0.0, -BIG)
    under = jnp.where(col < row, 0.0, -BIG)
    def operands(pair):
        at = slice(pair * LANES, (pair + 1) * LANES)
        q, k_new, v_new = query_ref[:, at], key_ref[:, at], value_ref[:, at]
        k_one, v_one = ck_ref[0, :, at], cv_ref[0, :, at]
        q_turn, k_turn, v_turn = (pltpu.roll(x, HEAD_DIM, 1) for x in (q, k_new, v_new))
        k_two, v_two = pltpu.roll(ck_ref[1, :, at], HEAD_DIM, 1), pltpu.roll(cv_ref[1, :, at], HEAD_DIM, 1)
        for side in range(2):
            mine, other = (low_one, high_one) if side == 0 else (high_one, low_one)
            in_mine = low if side == 0 else ~low
            held = jnp.where(in_mine, 1.0 - second, second).astype(jnp.bfloat16)
            queries = jnp.concatenate([(q * mine + q_turn * other) * held, asks], axis=1)
            keys = jnp.concatenate([k_one * mine + k_two * other, k_new * mine + k_turn * other], axis=0)
            keys = jnp.concatenate([keys, wrong], axis=1)
            values = jnp.concatenate([v_one * mine + v_two * other, v_new * mine + v_turn * other], axis=0)
            values = jnp.concatenate([values, ones], axis=1)
            yield queries, keys, values

    heads = [head for pair in range(2) for head in operands(pair)]
    steps = [(h, t) for h in range(len(heads)) for t in range(0, cap, STEP)]

    def score(step):
        h, t = step
        queries, keys, _ = heads[h]
        return lax.dot_general(
            queries[t * sources:(t + STEP) * sources], keys, (((1,), (1,)), ((), ())),
            preferred_element_type=jnp.float32,
        )

    ahead = score(steps[0])
    for at, (h, t) in enumerate(steps):
        scores = ahead
        if at + 1 < len(steps):
            ahead = score(steps[at + 1])
        rows = slice(t * sources, (t + STEP) * sources)
        bias = jnp.concatenate(
            [
                jnp.concatenate([upto if o <= k else under for o in range(cap)], axis=1)
                for k in range(t, t + STEP)
            ],
            axis=0,
        )
        old, fresh = scores[:, :depth], scores[:, depth:] + bias
        top = jnp.maximum(jnp.max(old, axis=1, keepdims=True), jnp.max(fresh, axis=1, keepdims=True))
        weights = jnp.concatenate(
            [jnp.exp(old - top).astype(jnp.bfloat16), jnp.exp(fresh - top).astype(jnp.bfloat16)], axis=1
        )
        mixed = jnp.dot(weights, heads[h][2], preferred_element_type=jnp.float32)
        mixed, total = mixed[:, :LANES], mixed[:, LANES:]
        turned = pltpu.roll(mixed, HEAD_DIM, 1)
        mixed = jnp.where(second[rows] == 1.0, turned, mixed) / total
        side = h % 2
        attn_ref[rows, h * HEAD_DIM:(h + 1) * HEAD_DIM] = mixed[
            :, side * HEAD_DIM:(side + 1) * HEAD_DIM
        ].astype(jnp.bfloat16)
    attn = attn_ref[...]
    source = iota((sources, 1), 0)
    lane_source = iota((1, sources), 1)
    which = iota((EDGE, 1), 0)
    last = jnp.full((EDGE, 1), -1, jnp.int32)
    for user in range(2):
        for k in range(cap):
            hit = jnp.where(meta[:, k:k + 1] == user, source * cap + k, -1)
            best = jnp.max(hit, axis=0, keepdims=True)
            last = jnp.where(which == user, jnp.maximum(last, best), last)
    picks = [
        jnp.where(lane_source * cap + k == last, 1.0, 0.0).astype(jnp.bfloat16) for k in range(cap)
    ]
    base = jnp.zeros((EDGE, width), jnp.float32)
    for k in range(cap):
        own = jnp.concatenate([got_ref[k], got_ref[cap + k]], axis=1)
        base = base + jnp.dot(picks[k], own, preferred_element_type=jnp.float32)
    base_ref[:EDGE] = base
    spot = iota((8, width), 1)
    base_ref[EDGE:] = jnp.where(spot == 2, ranks[0], jnp.where(spot == 3, ranks[1], 0.0))
    final = jnp.dot(jnp.concatenate(picks, axis=1), attn, preferred_element_type=jnp.float32).astype(jnp.bfloat16)
    me = lax.axis_index("heads")
    for group in range(groups):
        part = wo_ref[:, group * width:(group + 1) * width]
        edge_ref[group] = jnp.dot(final, part, preferred_element_type=jnp.float32).astype(jnp.bfloat16)
    leave = pltpu.make_async_copy(edge_ref, edge_hbm, sem)
    leave.start()
    for shift, out_ref in enumerate((own_ref, next_ref, across_ref, prev_ref)):
        group = lax.rem(me + shift, groups)
        part = wo_ref[:, pl.ds(pl.multiple_of(group * width, width), width)]
        out_ref[...] = jnp.dot(attn, part, preferred_element_type=jnp.float32).astype(jnp.bfloat16)
    leave.wait()


def state_kernel(owners, base_ref, terms_ref, out_ref):
    state = base_ref[:EDGE]
    ranks = base_ref[EDGE:EDGE + 1, :LANES].astype(jnp.int32)
    for g in range(terms_ref.shape[0]):
        state = state + terms_ref[g].astype(jnp.float32)
    line = iota((owners * 4, 1), 0)
    dest, part = line >> 2, line & 3
    value = jnp.zeros((owners * 4, LANES), jnp.float32)
    for user in range(2):
        for half in range(2):
            mine = (part == user * 2 + half) & (dest == ranks[:, 2 + user:3 + user])
            value = jnp.where(mine, state[user:user + 1, half * LANES:(half + 1) * LANES], value)
    out_ref[...] = value.astype(jnp.bfloat16)


def ranked_kernel(arrived_ref, out_ref):
    count = out_ref.shape[0]
    line = iota((1, 2 * count), 1)
    row = iota((count, 1), 0)
    for half in range(2):
        pick = jnp.where(line == 2 * row + half, 1.0, 0.0).astype(jnp.bfloat16)
        out_ref[:, half * LANES:(half + 1) * LANES] = jnp.dot(
            pick, arrived_ref[...], preferred_element_type=jnp.float32
        ).astype(jnp.bfloat16)


def refresh_kernel(got_ref, *refs):
    *term_refs, out_ref = refs
    slots, width = out_ref.shape
    _, sources, _ = got_ref.shape
    cap = slots // sources
    meta = got_ref[2 * cap].astype(jnp.float32)
    parts = []
    for k in range(cap):
        rows = slice(k * sources, (k + 1) * sources)
        mixed = sum(ref[rows, :].astype(jnp.float32) for ref in term_refs)
        own = jnp.concatenate([got_ref[k], got_ref[cap + k]], axis=1).astype(jnp.float32)
        parts.append(jnp.where(meta[:, k:k + 1] >= 0.0, own + mixed, 0.0).astype(jnp.bfloat16))
    updated = jnp.concatenate(parts, axis=0)
    line = iota((1, slots), 1)
    row = iota((slots, 1), 0)
    pick = jnp.where((line & (sources - 1)) * cap + line // sources == row, 1.0, 0.0).astype(jnp.bfloat16)
    out_ref[...] = jnp.dot(pick, updated, preferred_element_type=jnp.float32).astype(jnp.bfloat16)


def call(kernel, out, args, scratch=(), smem=(), hbm=(), out_hbm=None, cost=None, vmem=VMEM):
    specs = [
        pl.BlockSpec(memory_space=pltpu.SMEM if i in smem else pltpu.HBM if i in hbm else pltpu.VMEM)
        for i in range(len(args))
    ]
    return pl.pallas_call(
        kernel,
        out_shape=out,
        in_specs=specs,
        out_specs=jax.tree.map(
            lambda o: pl.BlockSpec(memory_space=pltpu.HBM if out_hbm == o.shape else pltpu.VMEM), out
        ),
        scratch_shapes=list(scratch),
        cost_estimate=cost,
        compiler_params=pltpu.CompilerParams(vmem_limit_bytes=vmem),
    )(*args)


def local(
    events, event_owner, event_user, cache_keys, cache_values, cache_len, user_rank,
    norm_gain, w_query, w_key, w_value, w_out,
):
    count, width = events.shape
    owners = lax.axis_size("users")
    groups = lax.axis_size("heads")
    cap = 2 * count // owners
    slots = owners * cap
    bf16 = jnp.bfloat16
    wide = groups * width
    sent = call(
        functools.partial(route_kernel, owners, cap),
        jax.ShapeDtypeStruct((owners * CHUNK, LANES), bf16),
        (
            event_owner.reshape(1, count), event_user.reshape(1, count), events,
            norm_gain.reshape(1, wide), cache_len, user_rank,
        ),
        scratch=[
            pltpu.VMEM((owners * CHUNK, LANES), bf16),
            pltpu.VMEM((1, count), jnp.int32),
            pltpu.VMEM((1, count), jnp.int32),
            pltpu.VMEM((count, width), bf16),
            pltpu.VMEM((1, wide), jnp.float32),
            pltpu.VMEM((1, 2), jnp.int32),
            pltpu.VMEM((1, 2), jnp.int32),
            pltpu.SemaphoreType.DMA((8,)),
        ],
        hbm=(0, 1, 2, 3, 4, 5),
        out_hbm=(owners * CHUNK, LANES),
        vmem=60 * 1024 * 1024,
    )
    got = lax.all_to_all(
        sent.reshape(owners, CHUNK // 2, 2, LANES), "users", split_axis=0, concat_axis=0, tiled=True
    )
    got = got.reshape(owners, CHUNK, LANES).transpose(1, 0, 2)
    own = got[:2 * cap]
    full = lax.all_to_all(
        jnp.broadcast_to(own, (groups,) + own.shape), "heads", split_axis=0, concat_axis=0, tiled=True
    )
    got, full = lax.optimization_barrier((got, full))
    own = got[:2 * cap]
    *terms, edge, base = call(
        attend_kernel,
        (jax.ShapeDtypeStruct((slots, width), bf16),) * groups
        + (
            jax.ShapeDtypeStruct((groups, EDGE, width), bf16),
            jax.ShapeDtypeStruct((EDGE + 8, width), jnp.float32),
        ),
        (
            full, got, w_query, w_key, w_value,
            cache_keys[0], cache_values[0], w_out,
        ),
        scratch=[
            pltpu.VMEM((slots, groups * width), bf16),
            pltpu.VMEM((slots, width), bf16),
            pltpu.VMEM((slots, width), bf16),
            pltpu.VMEM((slots, width), bf16),
            pltpu.VMEM((slots, width), bf16),
            pltpu.VMEM((groups, EDGE, width), bf16),
            pltpu.SemaphoreType.DMA,
        ],
        out_hbm=(groups, EDGE, width),
    )
    edge = lax.all_to_all(edge, "heads", split_axis=0, concat_axis=0, tiled=True)
    outgoing = call(
        functools.partial(state_kernel, owners),
        jax.ShapeDtypeStruct((owners * 4, LANES), bf16),
        (base, edge),
        cost=pl.CostEstimate(flops=PICK_FLOPS, bytes_accessed=1 << 20, transcendentals=0),
    )
    def passed(term, shift):
        return lax.ppermute(term, "heads", [(g, (g + shift) % groups) for g in range(groups)])

    across = passed(terms[2], 2)
    outgoing, one, three = lax.optimization_barrier((outgoing, terms[1], terms[3]))
    terms = [terms[0], passed(one, 1), across, passed(three, 3)]
    arrived = lax.all_to_all(
        outgoing.reshape(owners, 4, LANES), "users", split_axis=0, concat_axis=0, tiled=True
    )
    arrived, across = lax.optimization_barrier((arrived, across))
    terms[2] = across
    ranked = call(
        ranked_kernel,
        jax.ShapeDtypeStruct((owners * 2, width), bf16),
        (arrived.reshape(owners * 4, LANES),),
        cost=pl.CostEstimate(flops=PICK_FLOPS, bytes_accessed=1 << 20, transcendentals=0),
    )
    refreshed = call(
        refresh_kernel,
        jax.ShapeDtypeStruct((slots, width), bf16),
        (got, *terms),
        cost=pl.CostEstimate(flops=300_000_000, bytes_accessed=1 << 20, transcendentals=0),
    )
    return refreshed[None], ranked[None]


def solution(mesh):
    placed = (
        P("users", "heads"),
        P("users", None),
        P("users"),
        P("users", None, None, "heads"),
        P("users", None, None, "heads"),
        P("users", None),
        P("users", None),
        P(),
        P(None, "heads"),
        P(None, "heads"),
        P(None, "heads"),
        P("heads", None),
    )
    return jax.shard_map(
        local,
        mesh=mesh,
        in_specs=placed,
        out_specs=(P("users", None, "heads"), P("users", None, "heads")),
        check_vma=False,
    )
```

```python
import functools

import jax
import jax.numpy as jnp
from jax import lax
from jax.experimental import pallas as pl
from jax.experimental.pallas import tpu as pltpu
from jax.sharding import PartitionSpec as P

HEAD_DIM = 64
LANES = 128
CHUNK = 10
BIG = 1e30
PICK_FLOPS = 30_000_000_000
STEP = 2
PIECES = 32
EDGE = 16
VMEM = 16 * 1024 * 1024


def iota(shape, axis):
    return lax.broadcasted_iota(jnp.int32, shape, axis)


def route_kernel(
    owners, cap, owner_hbm, user_hbm, events_hbm, gain_hbm, len_hbm, rank_hbm,
    out_hbm, made_ref, owner_ref, user_ref, events_ref, gain_ref, len_ref, rank_ref, sems,
):
    copies = [
        pltpu.make_async_copy(source, target, sems.at[i])
        for i, (source, target) in enumerate(
            [
                (owner_hbm, owner_ref), (user_hbm, user_ref), (events_hbm, events_ref),
                (gain_hbm, gain_ref), (len_hbm, len_ref), (rank_hbm, rank_ref),
            ]
        )
    ]
    for copy in copies:
        copy.start()
    line = iota((owners * CHUNK, 1), 0)
    dest = jnp.floor((line.astype(jnp.float32) + 0.5) * (1.0 / CHUNK)).astype(jnp.int32)
    part = line - dest * CHUNK
    slot = jnp.where(part >= cap, part - cap, part)
    slot_line = jnp.where(part < 2 * cap, dest * CHUNK + slot, -1)
    user_line = jnp.where(part == 2 * cap, dest, -1)
    copies[0].wait()
    copies[1].wait()
    owner = owner_ref[...]
    user = user_ref[...]
    count = owner.shape[1]
    member = (iota((owners, count), 0) == owner).astype(jnp.bfloat16)
    same = lax.dot_general(member, member, (((0,), (0,)), ((), ())), preferred_element_type=jnp.float32)
    earlier = iota((count, count), 0) < iota((count, count), 1)
    rank = jnp.sum(jnp.where(earlier, same, 0.0), axis=0, keepdims=True).astype(jnp.int32)
    target = owner * CHUNK + rank
    named = jnp.where(iota((LANES, count), 0) == rank, user + 1, 0).astype(jnp.float32).astype(jnp.bfloat16)
    for copy in copies[2:]:
        copy.wait()
    me = lax.axis_index("users")
    piece = lax.rem(me, PIECES)
    gain = gain_ref[:, pl.ds(pl.multiple_of(lax.rem(piece, PIECES // 4) * LANES, LANES), LANES)]
    coarse = gain.astype(jnp.bfloat16).astype(jnp.float32)
    middle = (gain - coarse).astype(jnp.bfloat16).astype(jnp.float32)
    level = piece // (PIECES // 4)
    spare = jnp.where(level == 0, coarse, jnp.where(level == 1, middle, gain - coarse - middle))
    spare = jnp.where(level == 3, 0.0, spare)
    lane = iota((1, LANES), 1)
    back = jnp.zeros((1, LANES), jnp.int32)
    for user_at in range(2):
        length = len_ref[:, user_at:user_at + 1]
        back = jnp.where(lane == 3 * user_at, length >> 4, back)
        back = jnp.where(lane == 3 * user_at + 1, length & 15, back)
        back = jnp.where(lane == 3 * user_at + 2, rank_ref[:, user_at:user_at + 1], back)
    back = back.astype(jnp.float32)
    events = events_ref[...]
    half_lines = owners * CHUNK // 2
    leaving = []
    for half in range(2):
        at = slice(half * half_lines, (half + 1) * half_lines)
        pick = jnp.where((slot_line[at] == target) | (user_line[at] == owner), 1.0, 0.0).astype(jnp.bfloat16)
        rows = jnp.dot(pick, events, preferred_element_type=jnp.float32)
        users = lax.dot_general(pick, named, (((1,), (1,)), ((), ())), preferred_element_type=jnp.float32) - 1.0
        value = jnp.where(part[at] < cap, rows[:, :LANES], rows[:, LANES:])
        value = jnp.where(part[at] < 2 * cap, value, users)
        value = jnp.where(part[at] > 2 * cap, jnp.where(dest[at] == me, back, spare), value)
        made_ref[at, :] = value.astype(jnp.bfloat16)
        leaving.append(pltpu.make_async_copy(made_ref.at[at], out_hbm.at[at], sems.at[len(copies) + half]))
        leaving[half].start()
    for copy in leaving:
        copy.wait()


def attend_kernel(
    rows_ref, got_ref, wq_ref, wk_ref, wv_ref, ck_ref, cv_ref, wo_ref,
    own_ref, next_ref, across_ref, prev_ref, edge_hbm, base_ref, normed_ref, query_ref, key_ref, value_ref, attn_ref,
    edge_ref, sem,
):
    groups, parts, sources, _ = rows_ref.shape
    width = own_ref.shape[1]
    me_user = lax.axis_index("users")
    block = me_user // PIECES
    beside = jnp.where(block % 2 == 0, block + 1, block - 1)
    spare = got_ref[parts + 1, pl.ds(pl.multiple_of(beside * PIECES, PIECES), PIECES), :].astype(jnp.float32)
    fourth = PIECES // 4
    gain = spare[:fourth] + spare[fourth:2 * fourth] + spare[2 * fourth:3 * fourth]
    gain = jnp.concatenate([gain[g:g + 1] for g in range(fourth)], axis=1)
    back = got_ref[parts + 1, pl.ds(pl.multiple_of(block * PIECES, PIECES), PIECES), :].astype(jnp.float32)
    back = jnp.where(iota((PIECES, 1), 0) == lax.rem(me_user, PIECES), back, 0.0)
    back = jnp.sum(back, axis=0, keepdims=True)
    lengths = [back[:, 3 * user:3 * user + 1] * 16.0 + back[:, 3 * user + 1:3 * user + 2] for user in range(2)]
    ranks = [back[:, 3 * user + 2:3 * user + 3] for user in range(2)]
    cap = parts // 2
    slots = cap * sources
    depth = ck_ref.shape[1]
    for k in range(cap):
        wide = jnp.concatenate(
            [rows_ref[g, half * cap + k] for g in range(groups) for half in range(2)], axis=1
        ).astype(jnp.float32)
        mean = jnp.mean(wide * wide, axis=1, keepdims=True)
        normed = wide * lax.rsqrt(mean + 1e-05) * gain
        normed_ref[k * sources:(k + 1) * sources, :] = normed.astype(jnp.bfloat16)
    normed = normed_ref[...]
    query = jnp.dot(normed, wq_ref[...], preferred_element_type=jnp.float32).astype(jnp.bfloat16)
    query_ref[...] = query * jnp.bfloat16(HEAD_DIM ** -0.5)
    key_ref[...] = jnp.dot(normed, wk_ref[...], preferred_element_type=jnp.float32).astype(jnp.bfloat16)
    value_ref[...] = jnp.dot(normed, wv_ref[...], preferred_element_type=jnp.float32).astype(jnp.bfloat16)

    meta = got_ref[2 * cap].astype(jnp.float32)
    users = jnp.concatenate([meta[:, k:k + 1] for k in range(cap)], axis=0)
    second = jnp.where(users == 1.0, 1.0, 0.0)
    lane = iota((1, LANES), 1)
    low = lane < HEAD_DIM
    low_one = jnp.where(low, 1.0, 0.0).astype(jnp.bfloat16)
    high_one = jnp.where(low, 0.0, 1.0).astype(jnp.bfloat16)
    asks = jnp.where(lane == 0, 1.0 - second, jnp.where(lane == 1, second, 0.0)).astype(jnp.bfloat16)
    place = iota((depth, 1), 0).astype(jnp.float32)
    wrong_old = jnp.where(
        lane == 0,
        jnp.where(place < lengths[0], 0.0, -BIG),
        jnp.where(lane == 1, jnp.where(place < lengths[1], 0.0, -BIG), 0.0),
    )
    wrong_new = jnp.where(
        lane == 0,
        jnp.where(users == 0.0, 0.0, -BIG),
        jnp.where(lane == 1, jnp.where(users == 1.0, 0.0, -BIG), 0.0),
    )
    wrong = jnp.concatenate([wrong_old, wrong_new], axis=0).astype(jnp.bfloat16)
    ones = jnp.ones((depth + slots, LANES), jnp.bfloat16)
    row = iota((sources, sources), 0)
    col = iota((sources, sources), 1)
    upto = jnp.where(col <= row, 0.0, -BIG)
    under = jnp.where(col < row, 0.0, -BIG)
    def operands(pair):
        at = slice(pair * LANES, (pair + 1) * LANES)
        q, k_new, v_new = query_ref[:, at], key_ref[:, at], value_ref[:, at]
        k_one, v_one = ck_ref[0, :, at], cv_ref[0, :, at]
        q_turn, k_turn, v_turn = (pltpu.roll(x, HEAD_DIM, 1) for x in (q, k_new, v_new))
        k_two, v_two = pltpu.roll(ck_ref[1, :, at], HEAD_DIM, 1), pltpu.roll(cv_ref[1, :, at], HEAD_DIM, 1)
        for side in range(2):
            mine, other = (low_one, high_one) if side == 0 else (high_one, low_one)
            in_mine = low if side == 0 else ~low
            held = jnp.where(in_mine, 1.0 - second, second).astype(jnp.bfloat16)
            queries = jnp.concatenate([(q * mine + q_turn * other) * held, asks], axis=1)
            keys = jnp.concatenate([k_one * mine + k_two * other, k_new * mine + k_turn * other], axis=0)
            keys = jnp.concatenate([keys, wrong], axis=1)
            values = jnp.concatenate([v_one * mine + v_two * other, v_new * mine + v_turn * other], axis=0)
            values = jnp.concatenate([values, ones], axis=1)
            yield queries, keys, values

    heads = [head for pair in range(2) for head in operands(pair)]
    steps = [(h, t) for h in range(len(heads)) for t in range(0, cap, STEP)]

    def score(step):
        h, t = step
        queries, keys, _ = heads[h]
        return lax.dot_general(
            queries[t * sources:(t + STEP) * sources], keys, (((1,), (1,)), ((), ())),
            preferred_element_type=jnp.float32,
        )

    ahead = score(steps[0])
    for at, (h, t) in enumerate(steps):
        scores = ahead
        if at + 1 < len(steps):
            ahead = score(steps[at + 1])
        rows = slice(t * sources, (t + STEP) * sources)
        bias = jnp.concatenate(
            [
                jnp.concatenate([upto if o <= k else under for o in range(cap)], axis=1)
                for k in range(t, t + STEP)
            ],
            axis=0,
        )
        old, fresh = scores[:, :depth], scores[:, depth:] + bias
        top = jnp.maximum(jnp.max(old, axis=1, keepdims=True), jnp.max(fresh, axis=1, keepdims=True))
        weights = jnp.concatenate(
            [jnp.exp(old - top).astype(jnp.bfloat16), jnp.exp(fresh - top).astype(jnp.bfloat16)], axis=1
        )
        mixed = jnp.dot(weights, heads[h][2], preferred_element_type=jnp.float32)
        mixed, total = mixed[:, :LANES], mixed[:, LANES:]
        turned = pltpu.roll(mixed, HEAD_DIM, 1)
        mixed = jnp.where(second[rows] == 1.0, turned, mixed) / total
        side = h % 2
        attn_ref[rows, h * HEAD_DIM:(h + 1) * HEAD_DIM] = mixed[
            :, side * HEAD_DIM:(side + 1) * HEAD_DIM
        ].astype(jnp.bfloat16)
    attn = attn_ref[...]
    source = iota((sources, 1), 0)
    lane_source = iota((1, sources), 1)
    which = iota((EDGE, 1), 0)
    last = jnp.full((EDGE, 1), -1, jnp.int32)
    for user in range(2):
        for k in range(cap):
            hit = jnp.where(meta[:, k:k + 1] == user, source * cap + k, -1)
            best = jnp.max(hit, axis=0, keepdims=True)
            last = jnp.where(which == user, jnp.maximum(last, best), last)
    picks = [
        jnp.where(lane_source * cap + k == last, 1.0, 0.0).astype(jnp.bfloat16) for k in range(cap)
    ]
    base = jnp.zeros((EDGE, width), jnp.float32)
    for k in range(cap):
        own = jnp.concatenate([got_ref[k], got_ref[cap + k]], axis=1)
        base = base + jnp.dot(picks[k], own, preferred_element_type=jnp.float32)
    base_ref[:EDGE] = base
    spot = iota((8, width), 1)
    base_ref[EDGE:] = jnp.where(spot == 2, ranks[0], jnp.where(spot == 3, ranks[1], 0.0))
    final = jnp.dot(jnp.concatenate(picks, axis=1), attn, preferred_element_type=jnp.float32).astype(jnp.bfloat16)
    me = lax.axis_index("heads")
    for group in range(groups):
        part = wo_ref[:, group * width:(group + 1) * width]
        edge_ref[group] = jnp.dot(final, part, preferred_element_type=jnp.float32).astype(jnp.bfloat16)
    leave = pltpu.make_async_copy(edge_ref, edge_hbm, sem)
    leave.start()
    for shift, out_ref in enumerate((own_ref, next_ref, across_ref, prev_ref)):
        group = lax.rem(me + shift, groups)
        part = wo_ref[:, pl.ds(pl.multiple_of(group * width, width), width)]
        out_ref[...] = jnp.dot(attn, part, preferred_element_type=jnp.float32).astype(jnp.bfloat16)
    leave.wait()


def state_kernel(owners, base_ref, terms_ref, out_ref):
    state = base_ref[:EDGE]
    ranks = base_ref[EDGE:EDGE + 1, :LANES].astype(jnp.int32)
    for g in range(terms_ref.shape[0]):
        state = state + terms_ref[g].astype(jnp.float32)
    line = iota((owners * 4, 1), 0)
    dest, part = line >> 2, line & 3
    value = jnp.zeros((owners * 4, LANES), jnp.float32)
    for user in range(2):
        for half in range(2):
            mine = (part == user * 2 + half) & (dest == ranks[:, 2 + user:3 + user])
            value = jnp.where(mine, state[user:user + 1, half * LANES:(half + 1) * LANES], value)
    out_ref[...] = value.astype(jnp.bfloat16)


def ranked_kernel(arrived_ref, out_hbm, made_ref, sems):
    count = made_ref.shape[0]
    leaving = []
    for block in range(2):
        at = slice(block * count // 2, (block + 1) * count // 2)
        line = iota((1, count), 1)
        row = iota((count // 2, 1), 0)
        for half in range(2):
            pick = jnp.where(line == 2 * row + half, 1.0, 0.0).astype(jnp.bfloat16)
            made_ref[at, half * LANES:(half + 1) * LANES] = jnp.dot(
                pick, arrived_ref[block * count:(block + 1) * count], preferred_element_type=jnp.float32
            ).astype(jnp.bfloat16)
        leaving.append(pltpu.make_async_copy(made_ref.at[at], out_hbm.at[at], sems.at[block]))
        leaving[block].start()
    for copy in leaving:
        copy.wait()


def refresh_kernel(got_ref, *refs):
    *term_refs, out_hbm, made_ref, sems = refs
    slots, width = made_ref.shape
    _, sources, _ = got_ref.shape
    cap = slots // sources
    meta = got_ref[2 * cap].astype(jnp.float32)
    parts = []
    for k in range(cap):
        rows = slice(k * sources, (k + 1) * sources)
        mixed = sum(ref[rows, :].astype(jnp.float32) for ref in term_refs)
        own = jnp.concatenate([got_ref[k], got_ref[cap + k]], axis=1).astype(jnp.float32)
        parts.append(jnp.where(meta[:, k:k + 1] >= 0.0, own + mixed, 0.0).astype(jnp.bfloat16))
    updated = jnp.concatenate(parts, axis=0)
    line = iota((1, slots), 1)
    line = (line & (sources - 1)) * cap + line // sources
    leaving = []
    for half in range(2):
        at = slice(half * slots // 2, (half + 1) * slots // 2)
        row = iota((slots // 2, 1), 0) + half * slots // 2
        pick = jnp.where(line == row, 1.0, 0.0).astype(jnp.bfloat16)
        made_ref[at, :] = jnp.dot(pick, updated, preferred_element_type=jnp.float32).astype(jnp.bfloat16)
        leaving.append(pltpu.make_async_copy(made_ref.at[at], out_hbm.at[at], sems.at[half]))
        leaving[half].start()
    for copy in leaving:
        copy.wait()


def call(kernel, out, args, scratch=(), smem=(), hbm=(), out_hbm=None, cost=None, vmem=VMEM):
    specs = [
        pl.BlockSpec(memory_space=pltpu.SMEM if i in smem else pltpu.HBM if i in hbm else pltpu.VMEM)
        for i in range(len(args))
    ]
    return pl.pallas_call(
        kernel,
        out_shape=out,
        in_specs=specs,
        out_specs=jax.tree.map(
            lambda o: pl.BlockSpec(memory_space=pltpu.HBM if out_hbm == o.shape else pltpu.VMEM), out
        ),
        scratch_shapes=list(scratch),
        cost_estimate=cost,
        compiler_params=pltpu.CompilerParams(vmem_limit_bytes=vmem),
    )(*args)


def local(
    events, event_owner, event_user, cache_keys, cache_values, cache_len, user_rank,
    norm_gain, w_query, w_key, w_value, w_out,
):
    count, width = events.shape
    owners = lax.axis_size("users")
    groups = lax.axis_size("heads")
    cap = 2 * count // owners
    slots = owners * cap
    bf16 = jnp.bfloat16
    wide = groups * width
    sent = call(
        functools.partial(route_kernel, owners, cap),
        jax.ShapeDtypeStruct((owners * CHUNK, LANES), bf16),
        (
            event_owner.reshape(1, count), event_user.reshape(1, count), events,
            norm_gain.reshape(1, wide), cache_len, user_rank,
        ),
        scratch=[
            pltpu.VMEM((owners * CHUNK, LANES), bf16),
            pltpu.VMEM((1, count), jnp.int32),
            pltpu.VMEM((1, count), jnp.int32),
            pltpu.VMEM((count, width), bf16),
            pltpu.VMEM((1, wide), jnp.float32),
            pltpu.VMEM((1, 2), jnp.int32),
            pltpu.VMEM((1, 2), jnp.int32),
            pltpu.SemaphoreType.DMA((8,)),
        ],
        hbm=(0, 1, 2, 3, 4, 5),
        out_hbm=(owners * CHUNK, LANES),
        vmem=60 * 1024 * 1024,
    )
    got = lax.all_to_all(
        sent.reshape(owners, CHUNK // 2, 2, LANES), "users", split_axis=0, concat_axis=0, tiled=True
    )
    got = got.reshape(owners, CHUNK, LANES).transpose(1, 0, 2)
    own = got[:2 * cap]
    full = lax.all_to_all(
        jnp.broadcast_to(own, (groups,) + own.shape), "heads", split_axis=0, concat_axis=0, tiled=True
    )
    got, full = lax.optimization_barrier((got, full))
    own = got[:2 * cap]
    *terms, edge, base = call(
        attend_kernel,
        (jax.ShapeDtypeStruct((slots, width), bf16),) * groups
        + (
            jax.ShapeDtypeStruct((groups, EDGE, width), bf16),
            jax.ShapeDtypeStruct((EDGE + 8, width), jnp.float32),
        ),
        (
            full, got, w_query, w_key, w_value,
            cache_keys[0], cache_values[0], w_out,
        ),
        scratch=[
            pltpu.VMEM((slots, groups * width), bf16),
            pltpu.VMEM((slots, width), bf16),
            pltpu.VMEM((slots, width), bf16),
            pltpu.VMEM((slots, width), bf16),
            pltpu.VMEM((slots, width), bf16),
            pltpu.VMEM((groups, EDGE, width), bf16),
            pltpu.SemaphoreType.DMA,
        ],
        out_hbm=(groups, EDGE, width),
    )
    edge = lax.all_to_all(edge, "heads", split_axis=0, concat_axis=0, tiled=True)
    outgoing = call(
        functools.partial(state_kernel, owners),
        jax.ShapeDtypeStruct((owners * 4, LANES), bf16),
        (base, edge),
        cost=pl.CostEstimate(flops=PICK_FLOPS, bytes_accessed=1 << 20, transcendentals=0),
    )
    def passed(term, shift):
        return lax.ppermute(term, "heads", [(g, (g + shift) % groups) for g in range(groups)])

    across = passed(terms[2], 2)
    outgoing, one, three = lax.optimization_barrier((outgoing, terms[1], terms[3]))
    terms = [terms[0], passed(one, 1), across, passed(three, 3)]
    arrived = lax.all_to_all(
        outgoing.reshape(owners, 4, LANES), "users", split_axis=0, concat_axis=0, tiled=True
    )
    arrived, across = lax.optimization_barrier((arrived, across))
    terms[2] = across
    ranked = call(
        ranked_kernel,
        jax.ShapeDtypeStruct((owners * 2, width), bf16),
        (arrived.reshape(owners * 4, LANES),),
        scratch=[pltpu.VMEM((owners * 2, width), bf16), pltpu.SemaphoreType.DMA((2,))],
        out_hbm=(owners * 2, width),
        cost=pl.CostEstimate(flops=PICK_FLOPS, bytes_accessed=1 << 20, transcendentals=0),
    )
    refreshed = call(
        refresh_kernel,
        jax.ShapeDtypeStruct((slots, width), bf16),
        (got, *terms),
        scratch=[pltpu.VMEM((slots, width), bf16), pltpu.SemaphoreType.DMA((2,))],
        out_hbm=(slots, width),
        cost=pl.CostEstimate(flops=300_000_000, bytes_accessed=1 << 20, transcendentals=0),
    )
    return refreshed[None], ranked[None]


def solution(mesh):
    placed = (
        P("users", "heads"),
        P("users", None),
        P("users"),
        P("users", None, None, "heads"),
        P("users", None, None, "heads"),
        P("users", None),
        P("users", None),
        P(),
        P(None, "heads"),
        P(None, "heads"),
        P(None, "heads"),
        P("heads", None),
    )
    return jax.shard_map(
        local,
        mesh=mesh,
        in_specs=placed,
        out_specs=(P("users", None, "heads"), P("users", None, "heads")),
        check_vma=False,
    )
```
